32 devices in a mesh: dp: 8 (over y, x, core), tensor: 4 (over z).
Axes of the slice: x: 2, y: 2, z: 4, core: 2. Of those that a mesh axis runs over, the one named last changes fastest.
Arguments:
- tokens_in: bfloat16 [16384, 1024], P(('dp', 'tensor')), may hold values from -6 to 6
- segment_ids: int32 [16, 1024], P('dp'), may hold values from 0 to 3, as said below
- qkv_weight: bfloat16 [2, 3, 1024, 1024], P(None, None, 'dp', 'tensor'), may hold values from -0.1875 to 0.1875
- qv_bias: bfloat16 [2, 2, 1024], P(None, None, ('tensor', 'dp')), may hold values from -3 to 3
- out_weight: bfloat16 [2, 1024, 1024], P(None, 'tensor', 'dp'), may hold values from -0.75 to 0.75
- up_weight: bfloat16 [2, 1024, 4096], P(None, 'dp', 'tensor'), may hold values from -0.1875 to 0.1875
- up_bias: bfloat16 [2, 4096], P(None, ('tensor', 'dp')), may hold values from -3 to 3
- down_weight: bfloat16 [2, 4096, 1024], P(None, 'tensor', 'dp'), may hold values from -0.09375 to 0.09375
- row_params: bfloat16 [2, 6, 1024], P(None, None, ('dp', 'tensor'))
- cotangent: bfloat16 [16384, 1024], P(('dp', 'tensor')), may hold values from -6 to 6
Outputs:
- output: bfloat16 [16384, 1024], P(('dp', 'tensor'))
- grad_input: float32 [16384, 1024], P(('dp', 'tensor'))
- grad_qkv_weight: float32 [2, 3, 1024, 1024], P(None, None, 'dp', 'tensor')
- grad_qv_bias: float32 [2, 2, 1024], P(None, None, ('tensor', 'dp'))
- grad_out_weight: float32 [2, 1024, 1024], P(None, 'tensor', 'dp')
- grad_up_weight: float32 [2, 1024, 4096], P(None, 'dp', 'tensor')
- grad_up_bias: float32 [2, 4096], P(None, ('tensor', 'dp'))
- grad_down_weight: float32 [2, 4096, 1024], P(None, 'tensor', 'dp')
- grad_row_params: float32 [2, 6, 1024], P(None, None, ('dp', 'tensor'))
The draws below stay inside these ranges and needn't reach their ends.
Inputs may be any that keep to these rules, and one draw needn't show every extreme that they name: `segment_ids`: within each sequence the numbers never fall and start at 0; equal numbers mark one document.
All inputs are finite; a program needn't handle non-finite values.
Results may differ from the reference program's by a relative error of at most 0.022.
Values may be sent and summed in bfloat16 or wider, within the bound.
No kernel may reach another device: no remote copies, remote signals or barrier semaphores. Data moves between devices by JAX's collectives and lax.ppermute only.
A program may use at most 192 MiB of HBM per device.

```python
import math
import jax
import jax.numpy as jnp
from jax import lax

D = 1024
HEADS = 16
HEAD_DIM = 64
FF = 4096
LAYERS = 2
LEN = 1024
SEQ_DEV = 2
SEQS = 16
TOKENS = 16384


def draw_segment_ids(key, part):
    key = jax.random.fold_in(key, 3)
    key_whole, key_cuts, key_active = jax.random.split(key, 3)
    groups_total = SEQS // SEQ_DEV
    whole_pick = jax.random.randint(key_whole, (groups_total, 1), 0, SEQ_DEV)
    member = jnp.arange(SEQ_DEV, dtype=jnp.int32)[None, :]
    whole_row = (member == whole_pick).reshape(SEQS)
    dense_row = (member == (whole_pick + 1) % SEQ_DEV).reshape(SEQS)
    cut_keys = jax.random.split(key_cuts, SEQS)
    cut_places = jax.vmap(lambda single: jax.random.permutation(single, LEN - 1)[:3] + 1)(cut_keys)
    active = jax.random.randint(key_active, (SEQS, 3), 0, 2)
    active = jnp.where(dense_row[:, None], 1, active)
    active = jnp.where(whole_row[:, None], 0, active)
    position = jnp.arange(LEN, dtype=jnp.int32)
    passed = (position[None, None, :] >= cut_places[:, :, None]).astype(jnp.int32) * active[:, :, None]
    return jnp.sum(passed, axis=1).astype(jnp.int32)


def draw_row_params(key, part):
    key = jax.random.fold_in(key, 7)
    key_gain, key_shift = jax.random.split(key)
    gains = jax.random.uniform(key_gain, (LAYERS, 6, D), jnp.float32, 0.6, 1.4)
    shifts = 0.3 * jax.random.normal(key_shift, (LAYERS, 6, D), jnp.float32)
    gain_rows = (jnp.arange(6) % 3 == 0)[None, :, None]
    return jnp.where(gain_rows, gains, shifts).astype(jnp.bfloat16)


def level_of(own_key, shape, pieces, smallest, top_value):
    def one(dim, shards_of):
        draws = jax.random.uniform(jax.random.fold_in(jax.random.fold_in(own_key, 6), dim), (shards_of,), jnp.float32, smallest / len(pieces), top_value / len(pieces))
        return jnp.repeat(jnp.exp(draws), shape[dim] // shards_of).reshape((-1,) + (1,) * (len(shape) - dim - 1))

    loudness = one(*pieces[0])
    for cut in pieces[1:]:
        loudness = loudness * one(*cut)
    return loudness


def bell_draw(rng, dims, scale, reach, shards=(), kind=jnp.bfloat16):
    result = scale * jax.random.normal(rng, dims, jnp.float32)
    if shards:
        result = result * level_of(rng, dims, shards, -0.22, 0.18)
    return jnp.clip(result, -reach, reach).astype(kind)


def setup_inputs(seed: int = 0) -> dict:
    seeds = jax.random.split(jax.random.key(seed), 11)
    return {
        "tokens_in": bell_draw(seeds[0], (TOKENS, D), 1.0, 6.0, ((0, 32),)),
        "segment_ids": draw_segment_ids(jax.random.fold_in(seeds[10], 71), 0),
        "qkv_weight": bell_draw(seeds[2], (LAYERS, 3, D, D), D ** -0.5, 0.1875, ((2, 8), (3, 4))),
        "qv_bias": bell_draw(seeds[3], (LAYERS, 2, D), 0.5, 3.0, ((2, 32),)),
        "out_weight": bell_draw(seeds[4], (LAYERS, D, D), (D // 16) ** -0.5, 0.75, ((1, 4), (2, 8))),
        "up_weight": bell_draw(seeds[5], (LAYERS, D, FF), D ** -0.5, 0.1875, ((1, 8), (2, 4))),
        "up_bias": bell_draw(seeds[6], (LAYERS, FF), 0.5, 3.0, ((1, 32),)),
        "down_weight": bell_draw(seeds[7], (LAYERS, FF, D), FF ** -0.5, 0.09375, ((1, 4), (2, 8))),
        "row_params": draw_row_params(jax.random.fold_in(seeds[10], 71), 0),
        "cotangent": bell_draw(seeds[9], (TOKENS, D), 1.0, 6.0, ((0, 32),)),
    }


EPSILON = 1e-05
MASKED = -1e+30

@jax.custom_vjp
def low(v):
    return lax.optimization_barrier(v.astype(jnp.bfloat16)).astype(jnp.float32)

@jax.custom_vjp
def low_back(v):
    return v

def low_keep(v):
    return (low(v), None)

def low_pass(kept, grad):
    return (grad,)

def back_keep(v):
    return (v, None)

def back_low(kept, grad):
    return (low(grad),)
low.defvjp(low_keep, low_pass)
low_back.defvjp(back_keep, back_low)

def product(left_rows, right_matrix):
    return jnp.dot(left_rows, right_matrix, precision=lax.Precision.HIGHEST, preferred_element_type=jnp.float32)

def layer_norm(values, gain_row, shift_row):
    centre = lax.optimization_barrier(jnp.mean(values, axis=-1, keepdims=True))
    centred = values - centre
    spread = lax.optimization_barrier(jnp.mean(centred * centred, axis=-1, keepdims=True))
    return centred * lax.rsqrt(spread + EPSILON) * gain_row + shift_row

def gelu_tanh(values):
    return jax.nn.gelu(values, approximate=True)

def split_heads(matrix, sequences):
    return matrix.reshape(sequences, LEN, HEADS, HEAD_DIM)

def attend_sequence(inputs):
    queries, key_rows, value_rows, segment = inputs
    position = jnp.arange(LEN, dtype=jnp.int32)
    allowed = (position[:, None] >= position[None, :]) & (segment[:, None] == segment[None, :])
    distance = (position[:, None] - position[None, :]).astype(jnp.float32)
    slope_row = 2.0 ** (-8.0 * (jnp.arange(HEADS, dtype=jnp.float32) + 1.0) / HEADS)
    scores = jnp.einsum('qhd,khd->hqk', queries, key_rows, precision=lax.Precision.HIGHEST) * HEAD_DIM ** (-0.5)
    scores = scores - slope_row[:, None, None] * distance[None]
    scores = low_back(jnp.where(allowed[None], scores, MASKED))
    weights = low(jax.nn.softmax(scores, axis=-1))
    return jnp.einsum('hqk,khd->qhd', weights, value_rows, precision=lax.Precision.HIGHEST)

def forward(stream, segment, qkv_weight, qv_bias, out_weight, up_weight, up_bias, down_weight, row_params):
    sequences = segment.shape[0]
    for number in range(LAYERS):
        normed = low(layer_norm(stream, row_params[number, 0], row_params[number, 1]))
        queries = low(low_back(product(normed, qkv_weight[number, 0])) + qv_bias[number, 0])
        key_rows = low(low_back(product(normed, qkv_weight[number, 1])))
        value_rows = low(low_back(product(normed, qkv_weight[number, 2])) + qv_bias[number, 1])
        mixed = lax.map(jax.checkpoint(attend_sequence), (split_heads(queries, sequences), split_heads(key_rows, sequences), split_heads(value_rows, sequences), segment))
        attended = low(low_back(mixed.reshape(stream.shape)))
        stream = stream + (low_back(product(attended, out_weight[number])) + row_params[number, 2])
        normed_two = low(layer_norm(stream, row_params[number, 3], row_params[number, 4]))
        hidden = low(gelu_tanh(low_back(product(normed_two, up_weight[number])) + up_bias[number]))
        stream = stream + (low_back(product(hidden, down_weight[number])) + row_params[number, 5])
    return stream

def reference(tokens_in, segment_ids, qkv_weight, qv_bias, out_weight, up_weight, up_bias, down_weight, row_params, cotangent):
    params = (qkv_weight.astype(jnp.float32), qv_bias.astype(jnp.float32), out_weight.astype(jnp.float32), up_weight.astype(jnp.float32), up_bias.astype(jnp.float32), down_weight.astype(jnp.float32), row_params.astype(jnp.float32))
    group_size = math.gcd(segment_ids.shape[0], 4)
    group_count = segment_ids.shape[0] // group_size
    streams = tokens_in.astype(jnp.float32).reshape(group_count, group_size * LEN, D)
    segments = segment_ids.reshape(group_count, group_size, LEN)
    upstreams = cotangent.astype(jnp.float32).reshape(group_count, group_size * LEN, D)

    def one_group(totals, inputs):
        stream, segment, upstream = inputs

        def closed(stream_in, weights):
            return forward(stream_in, segment, weights[0], weights[1], weights[2], weights[3], weights[4], weights[5], weights[6])
        output, pullback = jax.vjp(closed, stream, params)
        stream_grad, weight_grads = pullback(upstream)
        return (jax.tree.map(jnp.add, totals, weight_grads), (output, stream_grad))
    zero_totals = jax.tree.map(jnp.zeros_like, params)
    totals, (outputs, stream_grads) = lax.scan(one_group, zero_totals, (streams, segments, upstreams))
    return (outputs.reshape(-1, D).astype(jnp.bfloat16), stream_grads.reshape(-1, D), totals[0], totals[1], totals[2], totals[3], totals[4], totals[5], totals[6])
```

```python
import functools

import jax
import jax.numpy as jnp
from jax import lax
from jax.experimental import pallas as pl
from jax.experimental.pallas import tpu as pltpu
from jax.sharding import PartitionSpec as P

HEADS = 16
HEAD_DIM = 64
LANES = 128
QBLK = 256

EPSILON = 1e-05
MASKED = -1e30
BOTH = ("dp", "tensor")
F32 = jnp.float32
BF16 = jnp.bfloat16


def dot_nt(left, right):
    return lax.dot_general(left, right, (((1,), (1,)), ((), ())), preferred_element_type=F32)


def dot_nn(left, right):
    return lax.dot_general(left, right, (((1,), (0,)), ((), ())), preferred_element_type=F32)


def dot_tn(left, right):
    return lax.dot_general(left, right, (((0,), (0,)), ((), ())), preferred_element_type=F32)


def fill_places(seg_col, seg_row, places, length):
    for first in range(0, length, QBLK):
        count = first + QBLK
        key_at = lax.broadcasted_iota(jnp.int32, (count, QBLK), 0)
        query_at = first + lax.broadcasted_iota(jnp.int32, (count, QBLK), 1)
        allowed = (key_at <= query_at) & (
            seg_col[0:count, :] == seg_row[:, first : first + QBLK]
        )
        places[0:count, first : first + QBLK] = jnp.where(
            allowed, key_at.astype(F32), MASKED
        )


def head_lanes(values, member):
    lane = lax.broadcasted_iota(jnp.int32, values.shape, 1)
    return jnp.where(lane // HEAD_DIM == member, values, jnp.zeros_like(values))


def forward_kernel(slopes, packed, seg_col, seg_row, mixed, places):
    group = pl.program_id(0)
    length = packed.shape[0]

    @pl.when(group == 0)
    def _():
        fill_places(seg_col, seg_row, places, length)

    scale = HEAD_DIM**-0.5
    values_t = packed[:, 2 * LANES : 3 * LANES].astype(F32).T.astype(BF16)
    keys = [
        head_lanes(packed[:, LANES : 2 * LANES].astype(F32), member).astype(BF16)
        for member in range(2)
    ]
    for first in range(0, length, QBLK):
        count = first + QBLK
        queries = (packed[first:count, 0:LANES].astype(F32) * scale).astype(BF16)
        parts = []
        for member in range(2):
            slope = slopes[group, member]
            scores = dot_nt(keys[member][0:count, :], queries)
            scores = scores + slope * places[0:count, first:count]
            top = jnp.max(scores, axis=0, keepdims=True)
            lifted = jnp.exp(scores - top)
            total = jnp.sum(lifted, axis=0, keepdims=True)
            rows = values_t[member * HEAD_DIM : (member + 1) * HEAD_DIM, 0:count]
            parts.append(dot_nn(rows, lifted.astype(BF16)) / total)
        mixed[first:count, :] = jnp.concatenate(parts, axis=0).T.astype(BF16)


def backward_kernel(
    slopes, packed, upstream, seg_col, seg_row, packed_grad, sums, places, key_grad, value_grad
):
    group = pl.program_id(0)
    length = packed.shape[0]

    @pl.when(group == 0)
    def _():
        fill_places(seg_col, seg_row, places, length)

    scale = HEAD_DIM**-0.5
    keys_f32 = packed[:, LANES : 2 * LANES].astype(F32)
    values_f32 = packed[:, 2 * LANES : 3 * LANES].astype(F32)
    keys = [head_lanes(keys_f32, member).astype(BF16) for member in range(2)]
    value_rows = [head_lanes(values_f32, member).astype(BF16) for member in range(2)]
    keys_t = (keys_f32 * scale).T.astype(BF16)
    query_sum = jnp.zeros((1, LANES), F32)
    for first in reversed(range(0, length, QBLK)):
        count = first + QBLK
        queries_f32 = packed[first:count, 0:LANES].astype(F32) * scale
        queries = queries_f32.astype(BF16)
        above_f32 = upstream[first:count, :].astype(F32)
        above = above_f32.astype(BF16)
        parts = []
        key_part = None
        value_part = None
        for member in range(2):
            slope = slopes[group, member]
            scores = dot_nt(keys[member][0:count, :], queries)
            scores = scores + slope * places[0:count, first:count]
            top = jnp.max(scores, axis=0, keepdims=True)
            lifted = jnp.exp(scores - top)
            total = jnp.sum(lifted, axis=0, keepdims=True)
            chances = lifted * (1.0 / total)
            chance_grad = dot_nt(value_rows[member][0:count, :], above)
            inner = jnp.sum(chance_grad * chances, axis=0, keepdims=True)
            score_grad = (chances * (chance_grad - inner)).astype(BF16)
            rows = keys_t[member * HEAD_DIM : (member + 1) * HEAD_DIM, 0:count]
            parts.append(dot_nn(rows, score_grad))
            key_term = dot_nn(score_grad, head_lanes(queries_f32, member).astype(BF16))
            value_term = dot_nn(chances.astype(BF16), head_lanes(above_f32, member).astype(BF16))
            key_part = key_term if member == 0 else key_part + key_term
            value_part = value_term if member == 0 else value_part + value_term
        query_grad = jnp.concatenate(parts, axis=0).T
        query_sum = query_sum + jnp.sum(query_grad, axis=0, keepdims=True)
        packed_grad[first:count, 0:LANES] = query_grad.astype(BF16)
        if count == length:
            key_grad[...] = key_part
            value_grad[...] = value_part
        else:
            key_grad[0:count, :] += key_part
            value_grad[0:count, :] += value_part
    packed_grad[:, LANES : 2 * LANES] = key_grad[...].astype(BF16)
    packed_grad[:, 2 * LANES : 3 * LANES] = value_grad[...].astype(BF16)
    sums[0:1, :] = query_sum
    sums[1:2, :] = jnp.sum(value_grad[...], axis=0, keepdims=True)


def attention_forward(packed, seg_col, seg_row, slopes):
    length, width = packed.shape
    groups = width // (3 * LANES)
    return pl.pallas_call(
        forward_kernel,
        grid=(groups,),
        in_specs=[
            pl.BlockSpec(memory_space=pltpu.SMEM),
            pl.BlockSpec((length, 3 * LANES), lambda g: (0, g)),
            pl.BlockSpec((length, 1), lambda g: (0, 0)),
            pl.BlockSpec((1, length), lambda g: (0, 0)),
        ],
        out_specs=pl.BlockSpec((length, LANES), lambda g: (0, g)),
        out_shape=jax.ShapeDtypeStruct((length, groups * LANES), BF16),
        scratch_shapes=[pltpu.VMEM((length, length), F32)],
        compiler_params=pltpu.CompilerParams(vmem_limit_bytes=40 * 2**20),
        cost_estimate=pl.CostEstimate(
            flops=groups * 2 * length * length * 256 * 3,
            bytes_accessed=groups * length * LANES * 8,
            transcendentals=groups * length * length * 2,
        ),
    )(slopes, packed, seg_col, seg_row)


def attention_backward(packed, upstream, seg_col, seg_row, slopes):
    length, width = packed.shape
    groups = width // (3 * LANES)
    return pl.pallas_call(
        backward_kernel,
        grid=(groups,),
        in_specs=[
            pl.BlockSpec(memory_space=pltpu.SMEM),
            pl.BlockSpec((length, 3 * LANES), lambda g: (0, g)),
            pl.BlockSpec((length, LANES), lambda g: (0, g)),
            pl.BlockSpec((length, 1), lambda g: (0, 0)),
            pl.BlockSpec((1, length), lambda g: (0, 0)),
        ],
        out_specs=[
            pl.BlockSpec((length, 3 * LANES), lambda g: (0, g)),
            pl.BlockSpec((None, 2, LANES), lambda g: (g, 0, 0)),
        ],
        out_shape=[
            jax.ShapeDtypeStruct((length, width), BF16),
            jax.ShapeDtypeStruct((groups, 2, LANES), F32),
        ],
        scratch_shapes=[
            pltpu.VMEM((length, length), F32),
            pltpu.VMEM((length, LANES), F32),
            pltpu.VMEM((length, LANES), F32),
        ],
        compiler_params=pltpu.CompilerParams(vmem_limit_bytes=48 * 2**20),
        cost_estimate=pl.CostEstimate(
            flops=groups * 2 * length * length * 256 * 8,
            bytes_accessed=groups * length * LANES * 14,
            transcendentals=groups * length * length * 2,
        ),
    )(slopes, packed, upstream, seg_col, seg_row)


def normalise(values):
    centred = values - jnp.mean(values, axis=-1, keepdims=True)
    spread = jnp.mean(centred * centred, axis=-1, keepdims=True)
    inverse = lax.rsqrt(spread + EPSILON)
    return centred * inverse, inverse


def layer_norm(values, gain_row, shift_row):
    return normalise(values)[0] * gain_row + shift_row


def norm_back(values, gain_row, upstream):
    unit, inverse = normalise(values)
    gain_grad = jnp.sum(upstream * unit, axis=0)
    shift_grad = jnp.sum(upstream, axis=0)
    inner = upstream * gain_row
    result = inverse * (
        inner
        - jnp.mean(inner, axis=-1, keepdims=True)
        - unit * jnp.mean(inner * unit, axis=-1, keepdims=True)
    )
    return result, gain_grad, shift_grad


def gelu_tanh(values):
    return jax.nn.gelu(values, approximate=True)


def bits_of(count):
    return [1 << place for place in range(count.bit_length() - 1)]


def body(
    dp_size,
    tensor_size,
    tokens_in,
    segment_ids,
    qkv_weight,
    qv_bias,
    out_weight,
    up_weight,
    up_bias,
    down_weight,
    row_params,
    cotangent,
):
    layers = qkv_weight.shape[0]
    shard_rows, features = tokens_in.shape
    spans = 2 * segment_ids.shape[0]
    inner_size = tensor_size // spans
    pairs = dp_size // 2
    devices = dp_size * tensor_size
    heads_half = HEADS // tensor_size // 2
    half_width = heads_half * HEAD_DIM
    wide = features // dp_size

    dp_at = lax.axis_index("dp")
    tensor_at = lax.axis_index("tensor")
    core = dp_at % 2
    pair = dp_at // 2
    span = tensor_at // inner_size
    inner = tensor_at % inner_size
    core_one = core == 1

    core_mask = tensor_size
    inner_masks = bits_of(inner_size)
    span_bits = bits_of(spans)
    pair_bits = bits_of(pairs)
    span_masks = {bit: bit * inner_size for bit in span_bits}
    pair_masks = {bit: bit * 2 * tensor_size for bit in pair_bits}

    def swap(values, mask):
        return lax.ppermute(values, BOTH, [(at, at ^ mask) for at in range(devices)])

    def crossed(at):
        at_core = (at // tensor_size) % 2
        at_span = (at % tensor_size) // inner_size
        return at if at_core == at_span % 2 else at ^ (core_mask | inner_size)

    def cross(values):
        return lax.ppermute(values, BOTH, [(at, crossed(at)) for at in range(devices)])

    def ordered(values, mask, is_high, axis):
        other = swap(values, mask)
        return jnp.concatenate(
            [jnp.where(is_high, other, values), jnp.where(is_high, values, other)], axis=axis
        )

    def group_rows(values):
        for mask in inner_masks:
            values = ordered(values, mask, (inner & mask) != 0, 0)
        return ordered(values, core_mask, core_one, 0)

    def group_sum(values):
        for mask in inner_masks + [core_mask]:
            low = values.astype(BF16)
            values = low.astype(F32) + swap(low, mask).astype(F32)
        return values

    high_spans = list(reversed(span_bits))
    orders = []
    for chosen in (pair_bits, list(reversed(pair_bits))):
        orders.append(
            [("span", bit) for bit in high_spans[:-1]]
            + [("pair", bit) for bit in chosen[:-1]]
            + [("span", bit) for bit in high_spans[-1:]]
            + [("pair", bit) for bit in chosen[-1:]]
        )

    def offsets(kind, order):
        found = [0]
        for step_kind, bit in order:
            if step_kind == kind:
                found = found + [place ^ bit for place in found]
        return found

    span_offsets = offsets("span", orders[0])
    pair_offsets = [offsets("pair", order) for order in orders]

    def mask_of(kind, bit):
        return span_masks[bit] if kind == "span" else pair_masks[bit]

    def to_local(values):
        axis = values.ndim - 1
        blocks = []
        for half in range(2):
            for offset in pair_offsets[half]:
                at = ((pair ^ offset) * 2 + half) * wide
                blocks.append(lax.dynamic_slice_in_dim(values, at, wide, axis))
        return jnp.concatenate(blocks, axis=axis)

    def from_local(values):
        axis = values.ndim - 1
        blocks = []
        for true_pair in range(pairs):
            for half in range(2):
                table = [0] * pairs
                for position, offset in enumerate(pair_offsets[half]):
                    table[offset] = position
                position = jnp.asarray(table, jnp.int32)[pair ^ true_pair]
                at = (half * pairs + position) * wide
                blocks.append(lax.dynamic_slice_in_dim(values, at, wide, axis))
        return jnp.concatenate(blocks, axis=axis)

    def fetch(halves, feature_axis):
        done = []
        for half, order in zip(halves, orders):
            for kind, bit in order:
                axis = feature_axis if kind == "pair" else 1 - feature_axis
                half = jnp.concatenate([half, swap(half, mask_of(kind, bit))], axis=axis)
            done.append(half)
        return jnp.concatenate(done, axis=feature_axis)

    def split_cores(low, high):
        mine = jnp.where(core_one, high, low)
        other = swap(jnp.where(core_one, low, high), core_mask)
        return jnp.where(core_one, other, mine), jnp.where(core_one, mine, other)

    def fetch_qkv(number):
        local = qkv_weight[number].transpose(1, 0, 2)
        rows = local.shape[0]
        low = local[:, :, :half_width].reshape(rows, 3 * half_width)
        high = local[:, :, half_width:].reshape(rows, 3 * half_width)
        return fetch(split_cores(low, high), 0)

    def fetch_columns(local):
        middle_at = local.shape[1] // 2
        return fetch(split_cores(local[:, :middle_at], local[:, middle_at:]), 0)

    def fetch_rows(local):
        middle_at = local.shape[0] // 2
        return fetch(split_cores(local[:middle_at], local[middle_at:]), 1)

    def reduce_grad(term, feature_axis):
        done = []
        part = features // 2
        for half, order in enumerate(orders):
            keep = term(half * part, part // 2).astype(BF16)
            send = term(half * part + part // 2, part // 2).astype(BF16)
            steps = list(reversed(order))
            for at, (kind, bit) in enumerate(steps):
                other = swap(send, mask_of(kind, bit))
                if at + 1 == len(steps):
                    done.append(keep.astype(F32) + other.astype(F32))
                    break
                next_kind = steps[at + 1][0]
                axis = feature_axis if next_kind == "pair" else 1 - feature_axis
                size = keep.shape[axis] // 2
                pieces = []
                for first in (0, size):
                    ours = lax.slice_in_dim(keep, first, first + size, axis=axis)
                    theirs = lax.slice_in_dim(other, first, first + size, axis=axis)
                    pieces.append((ours.astype(F32) + theirs.astype(F32)).astype(BF16))
                keep, send = pieces
        return done

    def join_cores(halves):
        first, second = halves
        mine = jnp.where(core_one, second, first)
        other = swap(jnp.where(core_one, first, second).astype(BF16), core_mask).astype(F32)
        return jnp.where(core_one, other, mine), jnp.where(core_one, mine, other)

    small_local = jnp.concatenate(
        [row_params.reshape(-1), qv_bias.reshape(-1), up_bias.reshape(-1)]
    )[None]
    small = small_local
    for mask in bits_of(devices):
        small = ordered(small, mask, (dp_at * tensor_size + tensor_at) & mask != 0, 0)
    row_size, qv_size = row_params.size, qv_bias.size
    rows_every = to_local(
        small[:, :row_size]
        .reshape(devices, layers, 6, -1)
        .transpose(1, 2, 0, 3)
        .reshape(layers, 6, features)
        .astype(F32)
    )

    def local_units(values, kinds):
        values = values.reshape(dp_size, spans, inner_size, layers, kinds, -1)
        values = lax.dynamic_slice_in_dim(values, core * pairs, pairs, 0)
        values = lax.dynamic_slice_in_dim(values, inner, 1, 2)[:, :, 0]
        blocks = [
            lax.dynamic_slice_in_dim(values, span ^ offset, 1, 1)[:, 0] for offset in span_offsets
        ]
        values = jnp.stack(blocks)
        return values.transpose(2, 3, 0, 1, 4).reshape(layers, kinds, -1).astype(F32)

    qv_local = local_units(small[:, row_size : row_size + qv_size], 2)
    up_bias_local = local_units(small[:, row_size + qv_size :], 1)[:, 0]

    span_at = jnp.stack([span ^ offset for offset in span_offsets])
    heads_at = (span_at * inner_size + inner)[:, None] * (2 * heads_half) + core * heads_half
    heads_at = heads_at + jnp.arange(heads_half, dtype=jnp.int32)[None]
    slopes = (2.0 ** (-8.0 * (heads_at.astype(F32) + 1.0) / HEADS)).reshape(-1, 2)
    joined_spans = max(1, LANES // half_width)

    def to_lanes(packed):
        if joined_spans == 1:
            return packed
        length = packed.shape[0]
        packed = packed.reshape(length, -1, joined_spans, 3, half_width)
        return packed.transpose(0, 1, 3, 2, 4).reshape(length, -1)

    def from_lanes(packed):
        if joined_spans == 1:
            return packed
        length = packed.shape[0]
        packed = packed.reshape(length, -1, 3, joined_spans, half_width)
        return packed.transpose(0, 1, 3, 2, 4).reshape(length, -1)

    own_segment = lax.dynamic_slice_in_dim(segment_ids, span // 2, 1, 0)
    seg_row = jnp.where(core == span % 2, own_segment, swap(own_segment, core_mask))
    seg_col = seg_row.reshape(-1, 1)

    stream = to_local(group_rows(cross(tokens_in))).astype(F32)
    upstream_low = to_local(group_rows(cross(cotangent)))

    stash = []
    for number in range(layers):
        rows = rows_every[number]
        qkv_full = fetch_qkv(number)
        out_full = fetch_rows(out_weight[number])
        up_full = fetch_columns(up_weight[number])
        down_full = fetch_rows(down_weight[number])
        normed = layer_norm(stream, rows[0], rows[1]).astype(BF16)
        qkv_bias = jnp.stack(
            [qv_local[number, 0], jnp.zeros_like(qv_local[number, 0]), qv_local[number, 1]]
        )
        qkv_bias = qkv_bias.reshape(3, spans, half_width).transpose(1, 0, 2).reshape(-1)
        packed = (jnp.dot(normed, qkv_full, preferred_element_type=F32) + qkv_bias).astype(BF16)
        packed = to_lanes(packed)
        attended = attention_forward(packed, seg_col, seg_row, slopes)
        middle = stream + (
            group_sum(jnp.dot(attended, out_full, preferred_element_type=F32)) + rows[2]
        )
        normed_two = layer_norm(middle, rows[3], rows[4]).astype(BF16)
        pre_gelu = (
            jnp.dot(normed_two, up_full, preferred_element_type=F32) + up_bias_local[number]
        )
        hidden = gelu_tanh(pre_gelu).astype(BF16)
        stash.append(
            (
                stream,
                normed,
                packed,
                attended,
                middle,
                normed_two,
                pre_gelu,
                hidden,
                qkv_full,
                out_full,
                up_full,
                down_full,
            )
        )
        stream = middle + (
            group_sum(jnp.dot(hidden, down_full, preferred_element_type=F32)) + rows[5]
        )

    def give_back(values):
        at = (core * inner_size + inner) * shard_rows
        return cross(lax.dynamic_slice_in_dim(from_local(values), at, shard_rows, 0))

    output = give_back(stream.astype(BF16))

    def total_sum(values):
        for bit in span_bits:
            values = values + swap(values, span_masks[bit])
        for bit in pair_bits:
            values = values + swap(values, pair_masks[bit])
        return values

    upstream = upstream_low.astype(F32)
    weight_grads = [None] * layers
    small_grads = [None] * layers
    for number in reversed(range(layers)):
        (
            stream_in,
            normed,
            packed,
            attended,
            middle,
            normed_two,
            pre_gelu,
            hidden,
            qkv_full,
            out_full,
            up_full,
            down_full,
        ) = stash[number]
        rows = rows_every[number]

        def columns_of(left, right):
            def term(first, count):
                return dot_tn(left, right[:, first : first + count])

            return term

        def rows_of(left, right):
            def term(first, count):
                return dot_tn(left[:, first : first + count], right)

            return term

        down_bias_grad = jnp.sum(upstream, axis=0)
        down_in = upstream.astype(BF16)
        hidden_grad = dot_nt(down_in, down_full)
        pre_grad = jax.vjp(gelu_tanh, pre_gelu)[1](hidden_grad)[0]
        up_bias_grad = jnp.sum(pre_grad, axis=0)
        pre_low = pre_grad.astype(BF16)
        normed_two_grad = group_sum(dot_nt(pre_low, up_full))
        down_grad = reduce_grad(columns_of(hidden, down_in), 1)
        up_grad = reduce_grad(rows_of(normed_two, pre_low), 0)
        middle_grad, gain_two_grad, shift_two_grad = norm_back(middle, rows[3], normed_two_grad)
        middle_grad = middle_grad + upstream
        out_bias_grad = jnp.sum(middle_grad, axis=0)
        out_in = middle_grad.astype(BF16)
        attended_grad = dot_nt(out_in, out_full).astype(BF16)
        out_grad = reduce_grad(columns_of(attended, out_in), 1)
        packed_grad, qv_sums = attention_backward(packed, attended_grad, seg_col, seg_row, slopes)
        packed_grad = from_lanes(packed_grad)
        normed_grad = group_sum(dot_nt(packed_grad, qkv_full))
        qkv_grad = reduce_grad(rows_of(normed, packed_grad), 0)
        stream_grad, gain_one_grad, shift_one_grad = norm_back(stream_in, rows[0], normed_grad)
        upstream = middle_grad + stream_grad

        row_grads = from_local(
            jnp.stack(
                [
                    gain_one_grad,
                    shift_one_grad,
                    out_bias_grad,
                    gain_two_grad,
                    shift_two_grad,
                    down_bias_grad,
                ]
            )
        )
        qv_units = qv_sums.transpose(1, 0, 2).reshape(2, spans, half_width)
        units = jnp.concatenate(
            [qv_units.transpose(1, 0, 2).reshape(spans, -1), up_bias_grad.reshape(spans, -1)],
            axis=1,
        )
        table = [0] * spans
        for position, offset in enumerate(span_offsets):
            table[offset] = position
        order_at = jnp.stack(
            [jnp.asarray(table, jnp.int32)[span ^ true_span] for true_span in range(spans)]
        )
        units = jnp.take(units, order_at, axis=0)
        small_grads[number] = total_sum(jnp.concatenate([row_grads.reshape(-1), units.reshape(-1)]))

        low, high = join_cores(qkv_grad)
        row_count = low.shape[0]
        qkv_own = jnp.concatenate(
            [low.reshape(row_count, 3, half_width), high.reshape(row_count, 3, half_width)], axis=2
        ).transpose(1, 0, 2)
        weight_grads[number] = (
            qkv_own,
            jnp.concatenate(join_cores(out_grad), axis=0),
            jnp.concatenate(join_cores(up_grad), axis=1),
            jnp.concatenate(join_cores(down_grad), axis=0),
        )

    summed = jnp.stack(small_grads)
    row_total = 6 * features
    own = features // devices
    row_summed = lax.dynamic_slice_in_dim(
        summed[:, :row_total].reshape(layers, 6, features),
        (dp_at * tensor_size + tensor_at) * own,
        own,
        2,
    )
    units = summed[:, row_total:].reshape(layers, spans, -1)
    units = lax.dynamic_slice_in_dim(units, span, 1, 1)[:, 0]
    other_units = swap(units, core_mask)
    units = jnp.where(core_one == (dp_at >= pairs), units, other_units)
    place = dp_at % pairs
    qv_part = units[:, : 2 * half_width].reshape(layers, 2, pairs, -1)
    up_part = units[:, 2 * half_width :].reshape(layers, pairs, -1)
    qv_own = lax.dynamic_slice_in_dim(qv_part, place, 1, 2)[:, :, 0]
    up_own = lax.dynamic_slice_in_dim(up_part, place, 1, 1)[:, 0]

    joined = [
        jnp.stack([weight_grads[number][member] for number in range(layers)]) for member in range(4)
    ]
    return (
        output,
        give_back(upstream.astype(BF16)).astype(F32),
        joined[0],
        qv_own,
        joined[1],
        joined[2],
        up_own,
        joined[3],
        row_summed,
    )


def solution(mesh):
    placed = (
        P(("dp", "tensor"), None),
        P("dp", None),
        P(None, None, "dp", "tensor"),
        P(None, None, ("tensor", "dp")),
        P(None, "tensor", "dp"),
        P(None, "dp", "tensor"),
        P(None, ("tensor", "dp")),
        P(None, "tensor", "dp"),
        P(None, None, ("dp", "tensor")),
        P(("dp", "tensor"), None),
    )
    return jax.shard_map(
        functools.partial(body, mesh.shape["dp"], mesh.shape["tensor"]),
        mesh=mesh,
        in_specs=placed,
        out_specs=(
            P(("dp", "tensor"), None),
            P(("dp", "tensor"), None),
            P(None, None, "dp", "tensor"),
            P(None, None, ("tensor", "dp")),
            P(None, "tensor", "dp"),
            P(None, "dp", "tensor"),
            P(None, ("tensor", "dp")),
            P(None, "tensor", "dp"),
            P(None, None, ("dp", "tensor")),
        ),
        check_vma=False,
    )
```

```python
import functools

import jax
import jax.numpy as jnp
from jax import lax
from jax.experimental import pallas as pl
from jax.experimental.pallas import tpu as pltpu
from jax.sharding import PartitionSpec as P

HEADS = 16
HEAD_DIM = 64
LANES = 128
QBLK = 256

EPSILON = 1e-05
MASKED = -1e30
BOTH = ("dp", "tensor")
F32 = jnp.float32
BF16 = jnp.bfloat16


def dot_nt(left, right):
    return lax.dot_general(left, right, (((1,), (1,)), ((), ())), preferred_element_type=F32)


def dot_nn(left, right):
    return lax.dot_general(left, right, (((1,), (0,)), ((), ())), preferred_element_type=F32)


def dot_tn(left, right):
    return lax.dot_general(left, right, (((0,), (0,)), ((), ())), preferred_element_type=F32)


def fill_places(seg_col, seg_row, places, length):
    for first in range(0, length, QBLK):
        count = first + QBLK
        key_at = lax.broadcasted_iota(jnp.int32, (count, QBLK), 0)
        query_at = first + lax.broadcasted_iota(jnp.int32, (count, QBLK), 1)
        allowed = (key_at <= query_at) & (
            seg_col[0:count, :] == seg_row[:, first : first + QBLK]
        )
        places[0:count, first : first + QBLK] = jnp.where(
            allowed, key_at.astype(F32), MASKED
        )


def head_lanes(values, member):
    lane = lax.broadcasted_iota(jnp.int32, values.shape, 1)
    return jnp.where(lane // HEAD_DIM == member, values, jnp.zeros_like(values))


def forward_kernel(slopes, query_in, key_in, value_in, seg_col, seg_row, mixed, places):
    group = pl.program_id(0)
    length = query_in.shape[0]

    @pl.when(group == 0)
    def _():
        fill_places(seg_col, seg_row, places, length)

    scale = HEAD_DIM**-0.5
    values_t = value_in[...].astype(F32).T.astype(BF16)
    keys = [
        head_lanes(key_in[...].astype(F32), member).astype(BF16)
        for member in range(2)
    ]
    for first in range(0, length, QBLK):
        count = first + QBLK
        queries = (query_in[first:count, :].astype(F32) * scale).astype(BF16)
        parts = []
        for member in range(2):
            slope = slopes[group, member]
            scores = dot_nt(keys[member][0:count, :], queries)
            scores = scores + slope * places[0:count, first:count]
            top = jnp.max(scores, axis=0, keepdims=True)
            lifted = jnp.exp(scores - top)
            total = jnp.sum(lifted, axis=0, keepdims=True)
            rows = values_t[member * HEAD_DIM : (member + 1) * HEAD_DIM, 0:count]
            parts.append(dot_nn(rows, lifted.astype(BF16)) / total)
        mixed[first:count, :] = jnp.concatenate(parts, axis=0).T.astype(BF16)


def backward_kernel(
    slopes,
    query_in,
    key_in,
    value_in,
    upstream,
    seg_col,
    seg_row,
    packed_grad,
    sums,
    places,
    key_grad,
    value_grad,
):
    group = pl.program_id(0)
    length = query_in.shape[0]

    @pl.when(group == 0)
    def _():
        fill_places(seg_col, seg_row, places, length)

    scale = HEAD_DIM**-0.5
    keys_f32 = key_in[...].astype(F32)
    values_f32 = value_in[...].astype(F32)
    keys = [head_lanes(keys_f32, member).astype(BF16) for member in range(2)]
    value_rows = [head_lanes(values_f32, member).astype(BF16) for member in range(2)]
    keys_t = (keys_f32 * scale).T.astype(BF16)
    query_sum = jnp.zeros((1, LANES), F32)
    for first in reversed(range(0, length, QBLK)):
        count = first + QBLK
        queries_f32 = query_in[first:count, :].astype(F32) * scale
        queries = queries_f32.astype(BF16)
        above_f32 = upstream[first:count, :].astype(F32)
        above = above_f32.astype(BF16)
        parts = []
        key_part = None
        value_part = None
        for member in range(2):
            slope = slopes[group, member]
            scores = dot_nt(keys[member][0:count, :], queries)
            scores = scores + slope * places[0:count, first:count]
            top = jnp.max(scores, axis=0, keepdims=True)
            lifted = jnp.exp(scores - top)
            total = jnp.sum(lifted, axis=0, keepdims=True)
            chances = lifted * (1.0 / total)
            chance_grad = dot_nt(value_rows[member][0:count, :], above)
            inner = jnp.sum(chance_grad * chances, axis=0, keepdims=True)
            score_grad = (chances * (chance_grad - inner)).astype(BF16)
            rows = keys_t[member * HEAD_DIM : (member + 1) * HEAD_DIM, 0:count]
            parts.append(dot_nn(rows, score_grad))
            key_term = dot_nn(score_grad, head_lanes(queries_f32, member).astype(BF16))
            value_term = dot_nn(chances.astype(BF16), head_lanes(above_f32, member).astype(BF16))
            key_part = key_term if member == 0 else key_part + key_term
            value_part = value_term if member == 0 else value_part + value_term
        query_grad = jnp.concatenate(parts, axis=0).T
        query_sum = query_sum + jnp.sum(query_grad, axis=0, keepdims=True)
        packed_grad[0, first:count, :] = query_grad.astype(BF16)
        if count == length:
            key_grad[...] = key_part
            value_grad[...] = value_part
        else:
            key_grad[0:count, :] += key_part
            value_grad[0:count, :] += value_part
    packed_grad[1] = key_grad[...].astype(BF16)
    packed_grad[2] = value_grad[...].astype(BF16)
    sums[0:1, :] = query_sum
    sums[1:2, :] = jnp.sum(value_grad[...], axis=0, keepdims=True)


def column_blocks(packed, length, groups):
    if len(packed) == 1:
        packed = packed * 3
        starts = (0, groups, 2 * groups)
    else:
        starts = (0, 0, 0)
    specs = [
        pl.BlockSpec((length, LANES), functools.partial(lambda start, g: (0, start + g), start))
        for start in starts
    ]
    return packed, specs


def attention_forward(packed, seg_col, seg_row, slopes):
    length = packed[0].shape[0]
    width = sum(array.shape[1] for array in packed) // 3
    groups = width // LANES
    packed, specs = column_blocks(packed, length, groups)
    block = pl.BlockSpec((length, LANES), lambda g: (0, g))
    return pl.pallas_call(
        forward_kernel,
        grid=(groups,),
        in_specs=[
            pl.BlockSpec(memory_space=pltpu.SMEM),
            *specs,
            pl.BlockSpec((length, 1), lambda g: (0, 0)),
            pl.BlockSpec((1, length), lambda g: (0, 0)),
        ],
        out_specs=block,
        out_shape=jax.ShapeDtypeStruct((length, width), BF16),
        scratch_shapes=[pltpu.VMEM((length, length), F32)],
        compiler_params=pltpu.CompilerParams(vmem_limit_bytes=40 * 2**20),
        cost_estimate=pl.CostEstimate(
            flops=groups * 2 * length * length * 256 * 5,
            bytes_accessed=groups * length * LANES * 8,
            transcendentals=groups * length * length * 2,
        ),
    )(slopes, *packed, seg_col, seg_row)


def attention_backward(packed, upstream, seg_col, seg_row, slopes):
    length, width = upstream.shape
    groups = width // LANES
    packed, specs = column_blocks(packed, length, groups)
    block = pl.BlockSpec((length, LANES), lambda g: (0, g))
    return pl.pallas_call(
        backward_kernel,
        grid=(groups,),
        in_specs=[
            pl.BlockSpec(memory_space=pltpu.SMEM),
            *specs,
            block,
            pl.BlockSpec((length, 1), lambda g: (0, 0)),
            pl.BlockSpec((1, length), lambda g: (0, 0)),
        ],
        out_specs=[
            pl.BlockSpec((3, length, LANES), lambda g: (0, 0, g)),
            pl.BlockSpec((None, 2, LANES), lambda g: (g, 0, 0)),
        ],
        out_shape=[
            jax.ShapeDtypeStruct((3, length, width), BF16),
            jax.ShapeDtypeStruct((groups, 2, LANES), F32),
        ],
        scratch_shapes=[
            pltpu.VMEM((length, length), F32),
            pltpu.VMEM((length, LANES), F32),
            pltpu.VMEM((length, LANES), F32),
        ],
        compiler_params=pltpu.CompilerParams(vmem_limit_bytes=48 * 2**20),
        cost_estimate=pl.CostEstimate(
            flops=groups * 2 * length * length * 256 * 8,
            bytes_accessed=groups * length * LANES * 14,
            transcendentals=groups * length * length * 2,
        ),
    )(slopes, *packed, upstream, seg_col, seg_row)


def merge_kernel(size, count, axis, first, second, joined, done):
    copies = []
    for at in range(count):
        for which, source in enumerate((first, second)):
            near = [slice(None), slice(None)]
            far = [slice(None), slice(None)]
            near[axis] = pl.ds(at * size, size)
            far[axis] = pl.ds((2 * at + which) * size, size)
            copies.append(
                pltpu.make_async_copy(
                    source.at[tuple(near)], joined.at[tuple(far)], done.at[2 * at + which]
                )
            )
    for copy in copies:
        copy.start()
    for copy in copies:
        copy.wait()


def merge(first, second, size, count, axis):
    shape = list(first.shape)
    shape[axis] *= 2
    grain = LANES if axis == 1 else 16
    if first.size < 2**20 or size % grain or shape[1] % LANES or shape[0] % 16:
        parts = []
        for at in range(count):
            for values in (first, second):
                parts.append(lax.slice_in_dim(values, at * size, (at + 1) * size, axis=axis))
        return jnp.concatenate(parts, axis=axis)
    anywhere = pl.BlockSpec(memory_space=pl.ANY)
    return pl.pallas_call(
        functools.partial(merge_kernel, size, count, axis),
        in_specs=[anywhere, anywhere],
        out_specs=anywhere,
        out_shape=jax.ShapeDtypeStruct(tuple(shape), first.dtype),
        scratch_shapes=[pltpu.SemaphoreType.DMA((2 * count,))],
        cost_estimate=pl.CostEstimate(
            flops=0, bytes_accessed=8 * first.size, transcendentals=0
        ),
    )(first, second)


def normalise(values):
    centred = values - jnp.mean(values, axis=-1, keepdims=True)
    spread = jnp.mean(centred * centred, axis=-1, keepdims=True)
    inverse = lax.rsqrt(spread + EPSILON)
    return centred * inverse, inverse


def layer_norm(values, gain_row, shift_row):
    return normalise(values)[0] * gain_row + shift_row


def norm_back(values, gain_row, upstream):
    unit, inverse = normalise(values)
    gain_grad = jnp.sum(upstream * unit, axis=0)
    shift_grad = jnp.sum(upstream, axis=0)
    inner = upstream * gain_row
    result = inverse * (
        inner
        - jnp.mean(inner, axis=-1, keepdims=True)
        - unit * jnp.mean(inner * unit, axis=-1, keepdims=True)
    )
    return result, gain_grad, shift_grad


def gelu_tanh(values):
    return jax.nn.gelu(values, approximate=True)


def bits_of(count):
    return [1 << place for place in range(count.bit_length() - 1)]


def body(
    dp_size,
    tensor_size,
    tokens_in,
    segment_ids,
    qkv_weight,
    qv_bias,
    out_weight,
    up_weight,
    up_bias,
    down_weight,
    row_params,
    cotangent,
):
    layers = qkv_weight.shape[0]
    shard_rows, features = tokens_in.shape
    spans = 2 * segment_ids.shape[0]
    inner_size = tensor_size // spans
    pairs = dp_size // 2
    devices = dp_size * tensor_size
    heads_half = HEADS // tensor_size // 2
    half_width = heads_half * HEAD_DIM

    dp_at = lax.axis_index("dp")
    tensor_at = lax.axis_index("tensor")
    core = dp_at % 2
    pair = dp_at // 2
    span = tensor_at // inner_size
    inner = tensor_at % inner_size
    core_one = core == 1

    core_mask = tensor_size
    inner_masks = bits_of(inner_size)
    span_bits = bits_of(spans)
    pair_bits = bits_of(pairs)
    span_masks = {bit: bit * inner_size for bit in span_bits}
    pair_masks = {bit: bit * 2 * tensor_size for bit in pair_bits}

    def swap(values, mask):
        return lax.ppermute(values, BOTH, [(at, at ^ mask) for at in range(devices)])

    def crossed(at):
        at_core = (at // tensor_size) % 2
        at_span = (at % tensor_size) // inner_size
        return at if at_core == at_span % 2 else at ^ (core_mask | inner_size)

    def cross(values):
        return lax.ppermute(values, BOTH, [(at, crossed(at)) for at in range(devices)])

    def ordered(values, mask, is_high, axis):
        other = swap(values, mask)
        return jnp.concatenate(
            [jnp.where(is_high, other, values), jnp.where(is_high, values, other)], axis=axis
        )

    def group_rows(values):
        for mask in inner_masks:
            values = ordered(values, mask, (inner & mask) != 0, 0)
        return ordered(values, core_mask, core_one, 0)

    def group_sum(values):
        for mask in inner_masks + [core_mask]:
            low = values.astype(BF16)
            values = low.astype(F32) + swap(low, mask).astype(F32)
        return values

    high_spans = [("span", bit) for bit in reversed(span_bits[1:])]
    turning = [("pair", bit) for bit in pair_bits]
    turning = turning[:1] + [("span", bit) for bit in span_bits[:1]] + turning[1:]
    orders = [high_spans + turning[by:] + turning[:by] for by in range(3)]

    def mask_of(kind, bit):
        return span_masks[bit] if kind == "span" else pair_masks[bit]

    def interleave(kind, bit, present, width, outer=1):
        lower = sum(1 for at_kind, at in present if at_kind == kind and at < bit)
        upper = sum(1 for at_kind, at in present if at_kind == kind and at > bit)
        return width << lower, (outer if kind == "span" else 1) << upper

    def halves_of(values, kind, bit, present, width, axis, outer):
        size, count = interleave(kind, bit, present, width, outer)
        halves = []
        for which in range(2):
            parts = [
                lax.slice_in_dim(
                    values, (2 * at + which) * size, (2 * at + which + 1) * size, axis=axis
                )
                for at in range(count)
            ]
            halves.append(parts[0] if count == 1 else jnp.concatenate(parts, axis=axis))
        return halves

    class Fetch:
        def __init__(self, block, feature_axis, order, outer=1):
            self.block = block
            self.outer = outer
            self.feature_axis = feature_axis
            self.order = orders[order]
            self.widths = {
                "pair": block.shape[feature_axis],
                "span": block.shape[1 - feature_axis] // outer,
            }
            self.place = 0

        def send(self):
            self.other = swap(self.block, mask_of(*self.order[self.place]))

        def take(self):
            kind, bit = self.order[self.place]
            axis = self.feature_axis if kind == "pair" else 1 - self.feature_axis
            present = self.order[: self.place]
            size, count = interleave(kind, bit, present, self.widths[kind], self.outer)
            self.block = merge(self.block, self.other, size, count, axis)
            self.place += 1
            if self.place < len(self.order):
                self.send()

    class Reduce:
        def __init__(self, feature_side, unit_side, feature_axis, order, outer=1):
            self.feature_axis = feature_axis
            self.outer = outer
            self.order = list(reversed(orders[order]))
            self.widths = {
                "pair": feature_side.shape[1] // pairs,
                "span": unit_side.shape[1] // spans // outer,
            }
            kind, bit = self.order[0]
            sides = {"pair": feature_side, "span": unit_side}
            found = []
            for part in halves_of(
                sides[kind], kind, bit, self.order[1:], self.widths[kind], 1, outer
            ):
                sides[kind] = part
                pair_of = [sides["pair"], sides["span"]]
                if feature_axis == 1:
                    pair_of.reverse()
                found.append(dot_tn(*pair_of).astype(BF16))
            self.keep, send = found
            self.other = swap(send, mask_of(kind, bit))
            self.place = 1

        def take(self):
            ours = self.keep
            theirs = self.other
            if self.place == len(self.order):
                self.result = ours.astype(F32) + theirs.astype(F32)
                self.place += 1
                return
            kind, bit = self.order[self.place]
            axis = self.feature_axis if kind == "pair" else 1 - self.feature_axis
            rest = self.order[self.place + 1 :]
            width = self.widths[kind]
            sums = [
                (first.astype(F32) + second.astype(F32)).astype(BF16)
                for first, second in zip(
                    halves_of(ours, kind, bit, rest, width, axis, self.outer),
                    halves_of(theirs, kind, bit, rest, width, axis, self.outer),
                )
            ]
            self.keep = sums[0]
            self.other = swap(sums[1], mask_of(kind, bit))
            self.place += 1

    def advance(values, chains):
        return tick(values, [chain for chain in chains if chain.place <= steps])

    def tick(values, chains):
        if not chains:
            return values
        values, others = lax.optimization_barrier((values, [chain.other for chain in chains]))
        for chain, other in zip(chains, others):
            chain.other = other
            chain.take()
        return values

    def to_local(values):
        axis = values.ndim - 1
        wide = features // pairs
        return jnp.concatenate(
            [
                lax.dynamic_slice_in_dim(values, (pair ^ offset) * wide, wide, axis)
                for offset in range(pairs)
            ],
            axis=axis,
        )

    from_local = to_local

    def split_cores(low, high, axis):
        mine = jnp.where(core_one, high, low)
        other = swap(jnp.where(core_one, low, high), core_mask)
        return jnp.concatenate(
            [jnp.where(core_one, other, mine), jnp.where(core_one, mine, other)], axis=axis
        )

    def blocks_of(number, which):
        if which == 0:
            local = qkv_weight[number].transpose(1, 0, 2)
            rows = local.shape[0]
            low = local[:, :, :half_width].reshape(rows, 3 * half_width)
            high = local[:, :, half_width:].reshape(rows, 3 * half_width)
            qkv = split_cores(low, high, 0)
            if number:
                found = [(qkv, 0, 2, 3)]
            else:
                found = [
                    (qkv[:, at * half_width : (at + 1) * half_width], 0, at, 1) for at in range(3)
                ]
            half = out_weight.shape[1] // 2
            out = split_cores(out_weight[number, :half], out_weight[number, half:], 1)
            return found + [(out, 1, 2, 1)]
        half = up_weight.shape[2] // 2
        up = split_cores(up_weight[number, :, :half], up_weight[number, :, half:], 0)
        half = down_weight.shape[1] // 2
        down = split_cores(down_weight[number, :half], down_weight[number, half:], 1)
        return [(up, 0, 0, 1), (down, 1, 1, 1)]

    def join_cores(values, feature_axis):
        size = values.shape[feature_axis] // 2
        first = lax.slice_in_dim(values, 0, size, axis=feature_axis)
        second = lax.slice_in_dim(values, size, 2 * size, axis=feature_axis)
        mine = jnp.where(core_one, second, first)
        other = swap(jnp.where(core_one, first, second).astype(BF16), core_mask).astype(F32)
        return jnp.where(core_one, other, mine), jnp.where(core_one, mine, other)

    first_blocks, first_rests = zip(*[(found[0], found[1:]) for found in blocks_of(0, 0)])
    (
        first_blocks,
        tokens_in,
        segment_ids,
        qkv_weight,
        qv_bias,
        out_weight,
        up_weight,
        up_bias,
        down_weight,
        row_params,
    ) = lax.optimization_barrier(
        (
            first_blocks,
            tokens_in,
            segment_ids,
            qkv_weight,
            qv_bias,
            out_weight,
            up_weight,
            up_bias,
            down_weight,
            row_params,
        )
    )

    small_local = jnp.concatenate(
        [row_params.reshape(-1), qv_bias.reshape(-1), up_bias.reshape(-1)]
    )[None]
    small = small_local
    for mask in bits_of(devices):
        small = ordered(small, mask, (dp_at * tensor_size + tensor_at) & mask != 0, 0)
    row_size, qv_size = row_params.size, qv_bias.size
    rows_every = to_local(
        small[:, :row_size]
        .reshape(devices, layers, 6, -1)
        .transpose(1, 2, 0, 3)
        .reshape(layers, 6, features)
        .astype(F32)
    )

    def local_units(values, kinds):
        values = values.reshape(dp_size, spans, inner_size, layers, kinds, -1)
        values = lax.dynamic_slice_in_dim(values, core * pairs, pairs, 0)
        values = lax.dynamic_slice_in_dim(values, inner, 1, 2)[:, :, 0]
        blocks = [
            lax.dynamic_slice_in_dim(values, span ^ offset, 1, 1)[:, 0] for offset in range(spans)
        ]
        values = jnp.stack(blocks)
        return values.transpose(2, 3, 0, 1, 4).reshape(layers, kinds, -1).astype(F32)

    qv_local = local_units(small[:, row_size : row_size + qv_size], 2)
    up_bias_local = local_units(small[:, row_size + qv_size :], 1)[:, 0]

    span_at = jnp.stack([span ^ offset for offset in range(spans)])
    heads_at = (span_at * inner_size + inner)[:, None] * (2 * heads_half) + core * heads_half
    heads_at = heads_at + jnp.arange(heads_half, dtype=jnp.int32)[None]
    slopes = (2.0 ** (-8.0 * (heads_at.astype(F32) + 1.0) / HEADS)).reshape(-1, 2)

    own_segment = lax.dynamic_slice_in_dim(segment_ids, span // 2, 1, 0)
    seg_row = jnp.where(core == span % 2, own_segment, swap(own_segment, core_mask))
    seg_col = seg_row.reshape(-1, 1)

    steps = len(orders[0])

    def fetches_of(blocks):
        return [Fetch(block, axis, order, outer) for block, axis, order, outer in blocks]

    stages = [fetches_of([(block, *rest) for block, rest in zip(first_blocks, first_rests)])]
    for chain in stages[0]:
        chain.send()
    fetches = [stages[0]]
    for number in range(layers):
        late = fetches_of(blocks_of(number, 1))
        fetches[number] = fetches[number] + late
        if number + 1 < layers:
            fetches.append(fetches_of(blocks_of(number + 1, 0)))
            late = late + fetches[number + 1]
        stages.append(late)
    for chain in stages[0]:
        chain.take()
    for before, after in zip(stages[:-1], stages[1:]):
        held = lax.optimization_barrier(
            ([chain.other for chain in before], [chain.block for chain in after])
        )
        for chain, other in zip(before, held[0]):
            chain.other = other
        for chain, block in zip(after, held[1]):
            chain.block = block
            chain.send()
    while stages[0][0].place < steps:
        for chain in stages[0]:
            chain.take()

    stream = to_local(group_rows(cross(tokens_in))).astype(F32)

    stash = []
    normed = layer_norm(stream, rows_every[0, 0], rows_every[0, 1]).astype(BF16)
    for number in range(layers):
        rows = rows_every[number]
        stage = stages[number + 1]
        weights = [chain.block for chain in fetches[number]]
        weights = weights[: len(weights) - 2] + [None, None]
        biases = (qv_local[number, 0], jnp.zeros_like(qv_local[number, 0]), qv_local[number, 1])
        if number:
            biases = (jnp.concatenate(biases),)
        packed = [
            (jnp.dot(normed, weight, preferred_element_type=F32) + bias).astype(BF16)
            for weight, bias in zip(weights[:-3], biases)
        ]
        if number == 0:
            packed = tick(packed, stage)
            packed, cotangent = lax.optimization_barrier((packed, cotangent))
            upstream_low = to_local(group_rows(cross(cotangent)))
        attended = attention_forward(packed, seg_col, seg_row, slopes)
        if number == 0:
            attended = tick(attended, stage)
        middle = stream + (
            group_sum(jnp.dot(attended, weights[-3], preferred_element_type=F32)) + rows[2]
        )
        normed_two = layer_norm(middle, rows[3], rows[4]).astype(BF16)
        while stage[0].place + 1 < steps:
            normed_two = tick(normed_two, stage)
        following = stages[number + 2] if number + 2 < len(stages) else []
        if following:
            normed_two = tick(normed_two, stage)
            weights_two, others = lax.optimization_barrier(
                ([chain.block for chain in stage], [chain.other for chain in following])
            )
            for chain, block in zip(stage, weights_two):
                chain.block = block
            for chain, other in zip(following, others):
                chain.other = other
                chain.take()
        else:
            for chain in stage:
                chain.take()
        weights = [chain.block for chain in fetches[number]]
        pre_gelu = (
            jnp.dot(normed_two, weights[-2], preferred_element_type=F32) + up_bias_local[number]
        )
        hidden = gelu_tanh(pre_gelu).astype(BF16)
        if following:
            hidden = tick(hidden, following)
        stash.append(
            (stream, normed, packed, attended, middle, normed_two, pre_gelu, hidden, weights)
        )
        stream = middle + (
            group_sum(jnp.dot(hidden, weights[-1], preferred_element_type=F32)) + rows[5]
        )
        if number + 1 < layers:
            after = rows_every[number + 1]
            normed = layer_norm(stream, after[0], after[1]).astype(BF16)
            if following[0].place + 1 < steps:
                normed = tick(normed, following)

    def give_back(values):
        at = (core * inner_size + inner) * shard_rows
        return cross(lax.dynamic_slice_in_dim(from_local(values), at, shard_rows, 0))

    output = give_back(stream.astype(BF16))

    upstream = upstream_low.astype(F32)
    reductions = [None] * layers
    small_grads = [None] * layers
    running = []
    for number in reversed(range(layers)):
        (
            stream_in,
            normed,
            packed,
            attended,
            middle,
            normed_two,
            pre_gelu,
            hidden,
            weights,
        ) = stash[number]
        rows = rows_every[number]
        apart = len(packed) == 3

        down_bias_grad = jnp.sum(upstream, axis=0)
        down_in = upstream.astype(BF16)
        down_chain = Reduce(down_in, hidden, 1, 1)
        hidden_grad = dot_nt(down_in, weights[-1])
        pre_grad = jax.vjp(gelu_tanh, pre_gelu)[1](hidden_grad)[0]
        up_bias_grad = jnp.sum(pre_grad, axis=0)
        pre_low = pre_grad.astype(BF16)
        pre_low = advance(pre_low, running)
        up_chain = Reduce(normed_two, pre_low, 0, 0)
        normed_two_grad = group_sum(dot_nt(pre_low, weights[-2]))
        normed_two_grad = advance(normed_two_grad, running)
        middle_grad, gain_two_grad, shift_two_grad = norm_back(middle, rows[3], normed_two_grad)
        middle_grad = middle_grad + upstream
        out_bias_grad = jnp.sum(middle_grad, axis=0)
        out_in = middle_grad.astype(BF16)
        attended_grad = dot_nt(out_in, weights[-3]).astype(BF16)
        attended_grad = advance(attended_grad, running + [down_chain])
        out_chain = Reduce(out_in, attended, 1, 2)
        packed_grad, qv_sums = attention_backward(packed, attended_grad, seg_col, seg_row, slopes)
        packed_grad = advance(packed_grad, running + [down_chain, up_chain, out_chain])
        if apart:
            qkv_chains = [Reduce(normed, packed_grad[at], 0, at) for at in range(3)]
            normed_grad = (
                dot_nt(packed_grad[0], weights[0])
                + dot_nt(packed_grad[1], weights[1])
                + dot_nt(packed_grad[2], weights[2])
            )
        else:
            beside = jnp.concatenate([packed_grad[at] for at in range(3)], axis=1)
            qkv_chains = [Reduce(normed, beside, 0, 2, 3)]
            normed_grad = dot_nt(beside, weights[0])
        normed_grad = group_sum(normed_grad)
        stream_grad, gain_one_grad, shift_one_grad = norm_back(stream_in, rows[0], normed_grad)
        upstream = middle_grad + stream_grad
        if number:
            upstream = advance(upstream, running + [down_chain, up_chain, out_chain])
        running = running + [down_chain, up_chain, out_chain] + qkv_chains
        reductions[number] = qkv_chains + [out_chain, up_chain, down_chain]

        row_grads = from_local(
            jnp.stack(
                [
                    gain_one_grad,
                    shift_one_grad,
                    out_bias_grad,
                    gain_two_grad,
                    shift_two_grad,
                    down_bias_grad,
                ]
            )
        )
        qv_units = qv_sums.transpose(1, 0, 2).reshape(2, spans, half_width)
        units = jnp.concatenate(
            [qv_units.transpose(1, 0, 2).reshape(spans, -1), up_bias_grad.reshape(spans, -1)],
            axis=1,
        )
        units = jnp.concatenate(
            [
                lax.dynamic_slice_in_dim(units, span ^ true_span, 1, 0)
                for true_span in range(spans)
            ],
            axis=0,
        )
        small_grads[number] = jnp.concatenate([row_grads.reshape(-1), units.reshape(-1)])
    def own_grads(number):
        found = [chain.result for chain in reductions[number]]
        low, high = join_cores(jnp.concatenate(found[:-3], axis=1), 0)
        row_count = low.shape[0]
        qkv_own = jnp.concatenate(
            [low.reshape(row_count, 3, half_width), high.reshape(row_count, 3, half_width)], axis=2
        ).transpose(1, 0, 2)
        return (
            qkv_own,
            jnp.concatenate(join_cores(found[-3], 1), axis=0),
            jnp.concatenate(join_cores(found[-2], 0), axis=1),
            jnp.concatenate(join_cores(found[-1], 1), axis=0),
        )

    weight_grads = [
        own_grads(number) if all(chain.place > steps for chain in reductions[number]) else None
        for number in range(layers)
    ]
    summed = jnp.stack(small_grads)
    upstream, summed, weight_grads = lax.optimization_barrier((upstream, summed, weight_grads))
    grad_input = give_back(upstream.astype(BF16))
    small_masks = [span_masks[bit] for bit in span_bits] + [pair_masks[bit] for bit in pair_bits]
    running = [chain for chain in running if chain.place <= steps]
    while running or small_masks:
        if small_masks:
            passed = swap(summed, small_masks[0])
        passed = advance(passed, running)
        if small_masks:
            summed = summed + passed
            small_masks = small_masks[1:]
        running = [chain for chain in running if chain.place <= steps]
    weight_grads = [
        own_grads(number) if weight_grads[number] is None else weight_grads[number]
        for number in range(layers)
    ]

    row_total = 6 * features
    own = features // devices
    row_summed = lax.dynamic_slice_in_dim(
        summed[:, :row_total].reshape(layers, 6, features),
        (dp_at * tensor_size + tensor_at) * own,
        own,
        2,
    )
    units = summed[:, row_total:].reshape(layers, spans, -1)
    units = lax.dynamic_slice_in_dim(units, span, 1, 1)[:, 0]
    other_units = swap(units, core_mask)
    units = jnp.where(core_one == (dp_at >= pairs), units, other_units)
    place = dp_at % pairs
    qv_part = units[:, : 2 * half_width].reshape(layers, 2, pairs, -1)
    up_part = units[:, 2 * half_width :].reshape(layers, pairs, -1)
    qv_own = lax.dynamic_slice_in_dim(qv_part, place, 1, 2)[:, :, 0]
    up_own = lax.dynamic_slice_in_dim(up_part, place, 1, 1)[:, 0]

    joined = [
        jnp.stack([weight_grads[number][member] for number in range(layers)]) for member in range(4)
    ]
    return (
        output,
        grad_input.astype(F32),
        joined[0],
        qv_own,
        joined[1],
        joined[2],
        up_own,
        joined[3],
        row_summed,
    )


def solution(mesh):
    placed = (
        P(("dp", "tensor"), None),
        P("dp", None),
        P(None, None, "dp", "tensor"),
        P(None, None, ("tensor", "dp")),
        P(None, "tensor", "dp"),
        P(None, "dp", "tensor"),
        P(None, ("tensor", "dp")),
        P(None, "tensor", "dp"),
        P(None, None, ("dp", "tensor")),
        P(("dp", "tensor"), None),
    )
    return jax.shard_map(
        functools.partial(body, mesh.shape["dp"], mesh.shape["tensor"]),
        mesh=mesh,
        in_specs=placed,
        out_specs=(
            P(("dp", "tensor"), None),
            P(("dp", "tensor"), None),
            P(None, None, "dp", "tensor"),
            P(None, None, ("tensor", "dp")),
            P(None, "tensor", "dp"),
            P(None, "dp", "tensor"),
            P(None, ("tensor", "dp")),
            P(None, "tensor", "dp"),
            P(None, None, ("dp", "tensor")),
        ),
        check_vma=False,
    )
```

```python
import functools

import jax
import jax.numpy as jnp
from jax import lax
from jax.experimental import pallas as pl
from jax.experimental.pallas import tpu as pltpu
from jax.sharding import PartitionSpec as P

HEADS = 16
HEAD_DIM = 64
LANES = 128
QBLK = 256

EPSILON = 1e-05
MASKED = -1e30
BOTH = ("dp", "tensor")
F32 = jnp.float32
BF16 = jnp.bfloat16


def dot_nt(left, right):
    return lax.dot_general(left, right, (((1,), (1,)), ((), ())), preferred_element_type=F32)


def dot_nn(left, right):
    return lax.dot_general(left, right, (((1,), (0,)), ((), ())), preferred_element_type=F32)


def dot_tn(left, right):
    return lax.dot_general(left, right, (((0,), (0,)), ((), ())), preferred_element_type=F32)


def fill_places(seg_col, seg_row, places, length):
    for first in range(0, length, QBLK):
        count = first + QBLK
        key_at = lax.broadcasted_iota(jnp.int32, (count, QBLK), 0)
        query_at = first + lax.broadcasted_iota(jnp.int32, (count, QBLK), 1)
        allowed = (key_at <= query_at) & (
            seg_col[0:count, :] == seg_row[:, first : first + QBLK]
        )
        places[0:count, first : first + QBLK] = jnp.where(
            allowed, key_at.astype(F32), MASKED
        )


def head_lanes(values, member):
    lane = lax.broadcasted_iota(jnp.int32, values.shape, 1)
    return jnp.where(lane // HEAD_DIM == member, values, jnp.zeros_like(values))


def forward_kernel(slopes, query_in, key_in, value_in, seg_col, seg_row, mixed, places):
    group = pl.program_id(0)
    length = query_in.shape[0]

    @pl.when(group == 0)
    def _():
        fill_places(seg_col, seg_row, places, length)

    scale = HEAD_DIM**-0.5
    values_t = value_in[...].astype(F32).T.astype(BF16)
    keys = [
        head_lanes(key_in[...].astype(F32), member).astype(BF16)
        for member in range(2)
    ]
    for first in range(0, length, QBLK):
        count = first + QBLK
        queries = (query_in[first:count, :].astype(F32) * scale).astype(BF16)
        parts = []
        for member in range(2):
            slope = slopes[group, member]
            scores = dot_nt(keys[member][0:count, :], queries)
            scores = scores + slope * places[0:count, first:count]
            top = jnp.max(scores, axis=0, keepdims=True)
            lifted = jnp.exp(scores - top)
            total = jnp.sum(lifted, axis=0, keepdims=True)
            rows = values_t[member * HEAD_DIM : (member + 1) * HEAD_DIM, 0:count]
            parts.append(dot_nn(rows, lifted.astype(BF16)) / total)
        mixed[first:count, :] = jnp.concatenate(parts, axis=0).T.astype(BF16)


def backward_kernel(
    slopes,
    query_in,
    key_in,
    value_in,
    upstream,
    seg_col,
    seg_row,
    packed_grad,
    sums,
    places,
    key_grad,
    value_grad,
):
    group = pl.program_id(0)
    length = query_in.shape[0]

    @pl.when(group == 0)
    def _():
        fill_places(seg_col, seg_row, places, length)

    scale = HEAD_DIM**-0.5
    keys_f32 = key_in[...].astype(F32)
    values_f32 = value_in[...].astype(F32)
    keys = [head_lanes(keys_f32, member).astype(BF16) for member in range(2)]
    value_rows = [head_lanes(values_f32, member).astype(BF16) for member in range(2)]
    keys_t = (keys_f32 * scale).T.astype(BF16)
    query_sum = jnp.zeros((1, LANES), F32)
    for first in reversed(range(0, length, QBLK)):
        count = first + QBLK
        queries_f32 = query_in[first:count, :].astype(F32) * scale
        queries = queries_f32.astype(BF16)
        above_f32 = upstream[first:count, :].astype(F32)
        above = above_f32.astype(BF16)
        parts = []
        key_part = None
        value_part = None
        for member in range(2):
            slope = slopes[group, member]
            scores = dot_nt(keys[member][0:count, :], queries)
            scores = scores + slope * places[0:count, first:count]
            top = jnp.max(scores, axis=0, keepdims=True)
            lifted = jnp.exp(scores - top)
            total = jnp.sum(lifted, axis=0, keepdims=True)
            chances = lifted * (1.0 / total)
            chance_grad = dot_nt(value_rows[member][0:count, :], above)
            inner = jnp.sum(chance_grad * chances, axis=0, keepdims=True)
            score_grad = (chances * (chance_grad - inner)).astype(BF16)
            rows = keys_t[member * HEAD_DIM : (member + 1) * HEAD_DIM, 0:count]
            parts.append(dot_nn(rows, score_grad))
            key_term = dot_nn(score_grad, head_lanes(queries_f32, member).astype(BF16))
            value_term = dot_nn(chances.astype(BF16), head_lanes(above_f32, member).astype(BF16))
            key_part = key_term if member == 0 else key_part + key_term
            value_part = value_term if member == 0 else value_part + value_term
        query_grad = jnp.concatenate(parts, axis=0).T
        query_sum = query_sum + jnp.sum(query_grad, axis=0, keepdims=True)
        packed_grad[0, first:count, :] = query_grad.astype(BF16)
        if count == length:
            key_grad[...] = key_part
            value_grad[...] = value_part
        else:
            key_grad[0:count, :] += key_part
            value_grad[0:count, :] += value_part
    packed_grad[1] = key_grad[...].astype(BF16)
    packed_grad[2] = value_grad[...].astype(BF16)
    sums[0:1, :] = query_sum
    sums[1:2, :] = jnp.sum(value_grad[...], axis=0, keepdims=True)


def column_blocks(packed, length, groups):
    if len(packed) == 1:
        packed = packed * 3
        starts = (0, groups, 2 * groups)
    else:
        starts = (0, 0, 0)
    specs = [
        pl.BlockSpec((length, LANES), functools.partial(lambda start, g: (0, start + g), start))
        for start in starts
    ]
    return packed, specs


def attention_forward(packed, seg_col, seg_row, slopes):
    length = packed[0].shape[0]
    width = sum(array.shape[1] for array in packed) // 3
    groups = width // LANES
    packed, specs = column_blocks(packed, length, groups)
    block = pl.BlockSpec((length, LANES), lambda g: (0, g))
    return pl.pallas_call(
        forward_kernel,
        grid=(groups,),
        in_specs=[
            pl.BlockSpec(memory_space=pltpu.SMEM),
            *specs,
            pl.BlockSpec((length, 1), lambda g: (0, 0)),
            pl.BlockSpec((1, length), lambda g: (0, 0)),
        ],
        out_specs=block,
        out_shape=jax.ShapeDtypeStruct((length, width), BF16),
        scratch_shapes=[pltpu.VMEM((length, length), F32)],
        compiler_params=pltpu.CompilerParams(vmem_limit_bytes=40 * 2**20),
        cost_estimate=pl.CostEstimate(
            flops=groups * 2 * length * length * 256 * 5,
            bytes_accessed=groups * length * LANES * 8,
            transcendentals=groups * length * length * 2,
        ),
    )(slopes, *packed, seg_col, seg_row)


def attention_backward(packed, upstream, seg_col, seg_row, slopes):
    length, width = upstream.shape
    groups = width // LANES
    packed, specs = column_blocks(packed, length, groups)
    block = pl.BlockSpec((length, LANES), lambda g: (0, g))
    return pl.pallas_call(
        backward_kernel,
        grid=(groups,),
        in_specs=[
            pl.BlockSpec(memory_space=pltpu.SMEM),
            *specs,
            block,
            pl.BlockSpec((length, 1), lambda g: (0, 0)),
            pl.BlockSpec((1, length), lambda g: (0, 0)),
        ],
        out_specs=[
            pl.BlockSpec((3, length, LANES), lambda g: (0, 0, g)),
            pl.BlockSpec((None, 2, LANES), lambda g: (g, 0, 0)),
        ],
        out_shape=[
            jax.ShapeDtypeStruct((3, length, width), BF16),
            jax.ShapeDtypeStruct((groups, 2, LANES), F32),
        ],
        scratch_shapes=[
            pltpu.VMEM((length, length), F32),
            pltpu.VMEM((length, LANES), F32),
            pltpu.VMEM((length, LANES), F32),
        ],
        compiler_params=pltpu.CompilerParams(vmem_limit_bytes=48 * 2**20),
        cost_estimate=pl.CostEstimate(
            flops=groups * 2 * length * length * 256 * 8,
            bytes_accessed=groups * length * LANES * 14,
            transcendentals=groups * length * length * 2,
        ),
    )(slopes, *packed, upstream, seg_col, seg_row)


def merge_kernel(axis, first, second, joined):
    size = first.shape[axis]
    for which, source in enumerate((first, second)):
        at = pl.ds(which * size, size)
        if axis == 0:
            joined[at, :] = source[...]
        else:
            joined[:, at] = source[...]


def merge(first, second, size, count, axis):
    shape = list(first.shape)
    shape[axis] *= 2
    grain = LANES if axis == 1 else 16
    if first.size < 2**20 or size % grain or shape[1] % (4 * LANES) or shape[0] % 64:
        parts = []
        for at in range(count):
            for values in (first, second):
                parts.append(lax.slice_in_dim(values, at * size, (at + 1) * size, axis=axis))
        return jnp.concatenate(parts, axis=axis)
    cuts = 4
    if axis == 0:
        block = (size, shape[1] // cuts)
        wide = (2 * size, shape[1] // cuts)
        place = lambda cut, at: (at, cut)
    else:
        block = (shape[0] // cuts, size)
        wide = (shape[0] // cuts, 2 * size)
        place = lambda cut, at: (cut, at)
    return pl.pallas_call(
        functools.partial(merge_kernel, axis),
        grid=(cuts, count),
        in_specs=[pl.BlockSpec(block, place)] * 2,
        out_specs=pl.BlockSpec(wide, place),
        out_shape=jax.ShapeDtypeStruct(tuple(shape), first.dtype),
        compiler_params=pltpu.CompilerParams(vmem_limit_bytes=24 * 2**20),
        cost_estimate=pl.CostEstimate(
            flops=0, bytes_accessed=8 * first.size, transcendentals=0
        ),
    )(first, second)


def normalise(values):
    centred = values - jnp.mean(values, axis=-1, keepdims=True)
    spread = jnp.mean(centred * centred, axis=-1, keepdims=True)
    inverse = lax.rsqrt(spread + EPSILON)
    return centred * inverse, inverse


def layer_norm(values, gain_row, shift_row):
    return normalise(values)[0] * gain_row + shift_row


def norm_back(values, gain_row, upstream):
    unit, inverse = normalise(values)
    gain_grad = jnp.sum(upstream * unit, axis=0)
    shift_grad = jnp.sum(upstream, axis=0)
    inner = upstream * gain_row
    result = inverse * (
        inner
        - jnp.mean(inner, axis=-1, keepdims=True)
        - unit * jnp.mean(inner * unit, axis=-1, keepdims=True)
    )
    return result, gain_grad, shift_grad


def gelu_tanh(values):
    return jax.nn.gelu(values, approximate=True)


def bits_of(count):
    return [1 << place for place in range(count.bit_length() - 1)]


def body(
    dp_size,
    tensor_size,
    tokens_in,
    segment_ids,
    qkv_weight,
    qv_bias,
    out_weight,
    up_weight,
    up_bias,
    down_weight,
    row_params,
    cotangent,
):
    layers = qkv_weight.shape[0]
    shard_rows, features = tokens_in.shape
    spans = 2 * segment_ids.shape[0]
    inner_size = tensor_size // spans
    pairs = dp_size // 2
    devices = dp_size * tensor_size
    heads_half = HEADS // tensor_size // 2
    half_width = heads_half * HEAD_DIM

    dp_at = lax.axis_index("dp")
    tensor_at = lax.axis_index("tensor")
    core = dp_at % 2
    pair = dp_at // 2
    span = tensor_at // inner_size
    inner = tensor_at % inner_size
    core_one = core == 1

    core_mask = tensor_size
    inner_masks = bits_of(inner_size)
    span_bits = bits_of(spans)
    pair_bits = bits_of(pairs)
    span_masks = {bit: bit * inner_size for bit in span_bits}
    pair_masks = {bit: bit * 2 * tensor_size for bit in pair_bits}

    def swap(values, mask):
        return lax.ppermute(values, BOTH, [(at, at ^ mask) for at in range(devices)])

    def crossed(at):
        at_core = (at // tensor_size) % 2
        at_span = (at % tensor_size) // inner_size
        return at if at_core == at_span % 2 else at ^ (core_mask | inner_size)

    def cross(values):
        return lax.ppermute(values, BOTH, [(at, crossed(at)) for at in range(devices)])

    def ordered(values, mask, is_high, axis):
        other = swap(values, mask)
        return jnp.concatenate(
            [jnp.where(is_high, other, values), jnp.where(is_high, values, other)], axis=axis
        )

    def group_rows(values):
        for mask in inner_masks:
            values = ordered(values, mask, (inner & mask) != 0, 0)
        return ordered(values, core_mask, core_one, 0)

    def group_sum(values):
        for mask in inner_masks + [core_mask]:
            low = values.astype(BF16)
            values = low.astype(F32) + swap(low, mask).astype(F32)
        return values

    high_spans = [("span", bit) for bit in reversed(span_bits[1:])]
    turning = [("pair", bit) for bit in pair_bits]
    turning = turning[:1] + [("span", bit) for bit in span_bits[:1]] + turning[1:]
    orders = [high_spans + turning[by:] + turning[:by] for by in range(3)]

    def mask_of(kind, bit):
        return span_masks[bit] if kind == "span" else pair_masks[bit]

    def interleave(kind, bit, present, width, outer=1):
        lower = sum(1 for at_kind, at in present if at_kind == kind and at < bit)
        upper = sum(1 for at_kind, at in present if at_kind == kind and at > bit)
        return width << lower, (outer if kind == "span" else 1) << upper

    def halves_of(values, kind, bit, present, width, axis, outer):
        size, count = interleave(kind, bit, present, width, outer)
        halves = []
        for which in range(2):
            parts = [
                lax.slice_in_dim(
                    values, (2 * at + which) * size, (2 * at + which + 1) * size, axis=axis
                )
                for at in range(count)
            ]
            halves.append(parts[0] if count == 1 else jnp.concatenate(parts, axis=axis))
        return halves

    class Fetch:
        def __init__(self, block, feature_axis, order, outer=1):
            self.block = block
            self.outer = outer
            self.feature_axis = feature_axis
            self.order = orders[order]
            self.widths = {
                "pair": block.shape[feature_axis],
                "span": block.shape[1 - feature_axis] // outer,
            }
            self.place = 0

        def send(self):
            self.other = swap(self.block, mask_of(*self.order[self.place]))

        def take(self):
            kind, bit = self.order[self.place]
            axis = self.feature_axis if kind == "pair" else 1 - self.feature_axis
            present = self.order[: self.place]
            size, count = interleave(kind, bit, present, self.widths[kind], self.outer)
            self.block = merge(self.block, self.other, size, count, axis)
            self.place += 1
            if self.place < len(self.order):
                self.send()

    class Reduce:
        def __init__(self, feature_side, unit_side, feature_axis, order, outer=1):
            self.feature_axis = feature_axis
            self.outer = outer
            self.order = list(reversed(orders[order]))
            self.widths = {
                "pair": feature_side.shape[1] // pairs,
                "span": unit_side.shape[1] // spans // outer,
            }
            kind, bit = self.order[0]
            sides = {"pair": feature_side, "span": unit_side}
            found = []
            for part in halves_of(
                sides[kind], kind, bit, self.order[1:], self.widths[kind], 1, outer
            ):
                sides[kind] = part
                pair_of = [sides["pair"], sides["span"]]
                if feature_axis == 1:
                    pair_of.reverse()
                found.append(dot_tn(*pair_of).astype(BF16))
            self.keep, send = found
            self.other = swap(send, mask_of(kind, bit))
            self.place = 1

        def take(self):
            ours = self.keep
            theirs = self.other
            if self.place == len(self.order):
                self.result = ours.astype(F32) + theirs.astype(F32)
                self.place += 1
                return
            kind, bit = self.order[self.place]
            axis = self.feature_axis if kind == "pair" else 1 - self.feature_axis
            rest = self.order[self.place + 1 :]
            width = self.widths[kind]
            sums = [
                (first.astype(F32) + second.astype(F32)).astype(BF16)
                for first, second in zip(
                    halves_of(ours, kind, bit, rest, width, axis, self.outer),
                    halves_of(theirs, kind, bit, rest, width, axis, self.outer),
                )
            ]
            self.keep = sums[0]
            self.other = swap(sums[1], mask_of(kind, bit))
            self.place += 1

    def advance(values, chains):
        return tick(values, [chain for chain in chains if chain.place <= steps])

    def tick(values, chains):
        if not chains:
            return values
        values, others = lax.optimization_barrier((values, [chain.other for chain in chains]))
        for chain, other in zip(chains, others):
            chain.other = other
            chain.take()
        return values

    def to_local(values):
        axis = values.ndim - 1
        wide = features // pairs
        return jnp.concatenate(
            [
                lax.dynamic_slice_in_dim(values, (pair ^ offset) * wide, wide, axis)
                for offset in range(pairs)
            ],
            axis=axis,
        )

    from_local = to_local

    def split_cores(low, high, axis):
        mine = jnp.where(core_one, high, low)
        other = swap(jnp.where(core_one, low, high), core_mask)
        return jnp.concatenate(
            [jnp.where(core_one, other, mine), jnp.where(core_one, mine, other)], axis=axis
        )

    def blocks_of(number, which):
        if which == 0:
            local = qkv_weight[number].transpose(1, 0, 2)
            rows = local.shape[0]
            low = local[:, :, :half_width].reshape(rows, 3 * half_width)
            high = local[:, :, half_width:].reshape(rows, 3 * half_width)
            qkv = split_cores(low, high, 0)
            if number:
                found = [(qkv, 0, 2, 3)]
            else:
                found = [
                    (qkv[:, at * half_width : (at + 1) * half_width], 0, at, 1) for at in range(3)
                ]
            half = out_weight.shape[1] // 2
            out = split_cores(out_weight[number, :half], out_weight[number, half:], 1)
            return found + [(out, 1, 2, 1)]
        half = up_weight.shape[2] // 2
        up = split_cores(up_weight[number, :, :half], up_weight[number, :, half:], 0)
        half = down_weight.shape[1] // 2
        down = split_cores(down_weight[number, :half], down_weight[number, half:], 1)
        return [(up, 0, 0, 1), (down, 1, 1, 1)]

    def join_cores(values, feature_axis):
        size = values.shape[feature_axis] // 2
        first = lax.slice_in_dim(values, 0, size, axis=feature_axis)
        second = lax.slice_in_dim(values, size, 2 * size, axis=feature_axis)
        mine = jnp.where(core_one, second, first)
        other = swap(jnp.where(core_one, first, second).astype(BF16), core_mask).astype(F32)
        return jnp.where(core_one, other, mine), jnp.where(core_one, mine, other)

    steps = len(orders[0])

    def fetches_of(blocks):
        return [Fetch(block, axis, order, outer) for block, axis, order, outer in blocks]

    early = fetches_of(blocks_of(0, 0))
    for chain in early:
        chain.send()
    others, rest = lax.optimization_barrier(
        (
            [chain.other for chain in early],
            (tokens_in, segment_ids, out_weight, qkv_weight, up_weight, down_weight),
        )
    )
    for chain, other in zip(early, others):
        chain.other = other
    tokens_in, segment_ids, out_weight, qkv_weight, up_weight, down_weight = rest
    small = jnp.concatenate(
        [row_params.reshape(-1), qv_bias.reshape(-1), up_bias.reshape(-1)]
    )[None]

    def small_hop(values, mask):
        return ordered(values, mask, (dp_at * tensor_size + tensor_at) & mask != 0, 0)

    small_hops = bits_of(devices)
    small = small_hop(small, small_hops[0])
    small = tick(small, early)
    tokens_here = cross(tokens_in)
    first_stage = fetches_of(blocks_of(0, 1))
    next_fetches = []
    if layers > 1:
        next_fetches = fetches_of(blocks_of(1, 0))
    first_stage = first_stage + next_fetches
    small = small_hop(small, small_hops[1])
    small, tokens_here, first_blocks = tick(
        (small, tokens_here, [chain.block for chain in first_stage]), early
    )
    for chain, block in zip(first_stage, first_blocks):
        chain.block = block
        chain.send()
    stream = group_rows(tokens_here)
    small = small_hop(small, small_hops[2])
    small, stream = tick((small, stream), early)
    stream = to_local(stream).astype(F32)
    for mask in small_hops[3:]:
        small = small_hop(small, mask)
    later_others, small = tick(([chain.other for chain in first_stage], small), early)
    for chain, other in zip(first_stage, later_others):
        chain.other = other
    while early[0].place < steps:
        for chain in early:
            chain.take()

    row_size, qv_size = row_params.size, qv_bias.size
    rows_every = to_local(
        small[:, :row_size]
        .reshape(devices, layers, 6, -1)
        .transpose(1, 2, 0, 3)
        .reshape(layers, 6, features)
        .astype(F32)
    )

    def local_units(values, kinds):
        values = values.reshape(dp_size, spans, inner_size, layers, kinds, -1)
        values = lax.dynamic_slice_in_dim(values, core * pairs, pairs, 0)
        values = lax.dynamic_slice_in_dim(values, inner, 1, 2)[:, :, 0]
        blocks = [
            lax.dynamic_slice_in_dim(values, span ^ offset, 1, 1)[:, 0] for offset in range(spans)
        ]
        values = jnp.stack(blocks)
        return values.transpose(2, 3, 0, 1, 4).reshape(layers, kinds, -1).astype(F32)

    qv_local = local_units(small[:, row_size : row_size + qv_size], 2)
    up_bias_local = local_units(small[:, row_size + qv_size :], 1)[:, 0]

    span_at = jnp.stack([span ^ offset for offset in range(spans)])
    heads_at = (span_at * inner_size + inner)[:, None] * (2 * heads_half) + core * heads_half
    heads_at = heads_at + jnp.arange(heads_half, dtype=jnp.int32)[None]
    slopes = (2.0 ** (-8.0 * (heads_at.astype(F32) + 1.0) / HEADS)).reshape(-1, 2)

    own_segment = lax.dynamic_slice_in_dim(segment_ids, span // 2, 1, 0)
    seg_row = jnp.where(core == span % 2, own_segment, swap(own_segment, core_mask))
    seg_col = seg_row.reshape(-1, 1)

    fetches = [early + first_stage[:2], first_stage[2:]]
    stages = [early, first_stage]
    for number in range(1, layers):
        late = fetches_of(blocks_of(number, 1))
        fetches[number] = fetches[number] + late
        if number + 1 < layers:
            fetches.append(fetches_of(blocks_of(number + 1, 0)))
            late = late + fetches[number + 1]
        stages.append(late)
    for before, after in zip(stages[1:-1], stages[2:]):
        held = lax.optimization_barrier(
            ([chain.other for chain in before], [chain.block for chain in after])
        )
        for chain, other in zip(before, held[0]):
            chain.other = other
        for chain, block in zip(after, held[1]):
            chain.block = block
            chain.send()

    stash = []
    normed = layer_norm(stream, rows_every[0, 0], rows_every[0, 1]).astype(BF16)
    for number in range(layers):
        rows = rows_every[number]
        stage = stages[number + 1]
        weights = [chain.block for chain in fetches[number]]
        weights = weights[: len(weights) - 2] + [None, None]
        biases = (qv_local[number, 0], jnp.zeros_like(qv_local[number, 0]), qv_local[number, 1])
        if number:
            biases = (jnp.concatenate(biases),)
        packed = [
            (jnp.dot(normed, weight, preferred_element_type=F32) + bias).astype(BF16)
            for weight, bias in zip(weights[:-3], biases)
        ]
        if number == 0:
            packed = tick(packed, stage)
            packed, cotangent = lax.optimization_barrier((packed, cotangent))
            upstream_low = to_local(group_rows(cross(cotangent)))
        attended = attention_forward(packed, seg_col, seg_row, slopes)
        if number == 0:
            attended = tick(attended, stage)
        middle = stream + (
            group_sum(jnp.dot(attended, weights[-3], preferred_element_type=F32)) + rows[2]
        )
        normed_two = layer_norm(middle, rows[3], rows[4]).astype(BF16)
        while stage[0].place + 1 < steps:
            normed_two = tick(normed_two, stage)
        following = stages[number + 2] if number + 2 < len(stages) else []
        if following:
            normed_two = tick(normed_two, stage)
            weights_two, others = lax.optimization_barrier(
                ([chain.block for chain in stage], [chain.other for chain in following])
            )
            for chain, block in zip(stage, weights_two):
                chain.block = block
            for chain, other in zip(following, others):
                chain.other = other
                chain.take()
        else:
            for chain in stage:
                chain.take()
        weights = [chain.block for chain in fetches[number]]
        pre_gelu = (
            jnp.dot(normed_two, weights[-2], preferred_element_type=F32) + up_bias_local[number]
        )
        hidden = gelu_tanh(pre_gelu).astype(BF16)
        if following:
            hidden = tick(hidden, following)
        stash.append(
            (stream, normed, packed, attended, middle, normed_two, pre_gelu, hidden, weights)
        )
        stream = middle + (
            group_sum(jnp.dot(hidden, weights[-1], preferred_element_type=F32)) + rows[5]
        )
        if number + 1 < layers:
            after = rows_every[number + 1]
            normed = layer_norm(stream, after[0], after[1]).astype(BF16)
            if following[0].place + 1 < steps:
                normed = tick(normed, following)

    def give_back(values):
        at = (core * inner_size + inner) * shard_rows
        return cross(lax.dynamic_slice_in_dim(from_local(values), at, shard_rows, 0))

    output = give_back(stream.astype(BF16))

    upstream = upstream_low.astype(F32)
    reductions = [None] * layers
    small_grads = [None] * layers
    running = []
    for number in reversed(range(layers)):
        (
            stream_in,
            normed,
            packed,
            attended,
            middle,
            normed_two,
            pre_gelu,
            hidden,
            weights,
        ) = stash[number]
        rows = rows_every[number]
        apart = len(packed) == 3

        down_bias_grad = jnp.sum(upstream, axis=0)
        down_in = upstream.astype(BF16)
        down_chain = Reduce(down_in, hidden, 1, 1)
        hidden_grad = dot_nt(down_in, weights[-1])
        pre_grad = jax.vjp(gelu_tanh, pre_gelu)[1](hidden_grad)[0]
        up_bias_grad = jnp.sum(pre_grad, axis=0)
        pre_low = pre_grad.astype(BF16)
        pre_low = advance(pre_low, running)
        up_chain = Reduce(normed_two, pre_low, 0, 0)
        normed_two_grad = group_sum(dot_nt(pre_low, weights[-2]))
        normed_two_grad = advance(normed_two_grad, running)
        middle_grad, gain_two_grad, shift_two_grad = norm_back(middle, rows[3], normed_two_grad)
        middle_grad = middle_grad + upstream
        out_bias_grad = jnp.sum(middle_grad, axis=0)
        out_in = middle_grad.astype(BF16)
        attended_grad = dot_nt(out_in, weights[-3]).astype(BF16)
        attended_grad = advance(attended_grad, running + [down_chain])
        out_chain = Reduce(out_in, attended, 1, 2)
        packed_grad, qv_sums = attention_backward(packed, attended_grad, seg_col, seg_row, slopes)
        packed_grad = advance(packed_grad, running + [down_chain, up_chain, out_chain])
        if apart:
            qkv_chains = [Reduce(normed, packed_grad[at], 0, at) for at in range(3)]
            normed_grad = (
                dot_nt(packed_grad[0], weights[0])
                + dot_nt(packed_grad[1], weights[1])
                + dot_nt(packed_grad[2], weights[2])
            )
        else:
            beside = jnp.concatenate([packed_grad[at] for at in range(3)], axis=1)
            qkv_chains = [Reduce(normed, beside, 0, 2, 3)]
            normed_grad = dot_nt(beside, weights[0])
        normed_grad = group_sum(normed_grad)
        stream_grad, gain_one_grad, shift_one_grad = norm_back(stream_in, rows[0], normed_grad)
        upstream = middle_grad + stream_grad
        if number:
            upstream = advance(upstream, running + [down_chain, up_chain, out_chain])
        running = running + [down_chain, up_chain, out_chain] + qkv_chains
        reductions[number] = qkv_chains + [out_chain, up_chain, down_chain]

        row_grads = from_local(
            jnp.stack(
                [
                    gain_one_grad,
                    shift_one_grad,
                    out_bias_grad,
                    gain_two_grad,
                    shift_two_grad,
                    down_bias_grad,
                ]
            )
        )
        qv_units = qv_sums.transpose(1, 0, 2).reshape(2, spans, half_width)
        units = jnp.concatenate(
            [qv_units.transpose(1, 0, 2).reshape(spans, -1), up_bias_grad.reshape(spans, -1)],
            axis=1,
        )
        units = jnp.concatenate(
            [
                lax.dynamic_slice_in_dim(units, span ^ true_span, 1, 0)
                for true_span in range(spans)
            ],
            axis=0,
        )
        small_grads[number] = jnp.concatenate([row_grads.reshape(-1), units.reshape(-1)])
    def own_grads(number):
        found = [chain.result for chain in reductions[number]]
        low, high = join_cores(jnp.concatenate(found[:-3], axis=1), 0)
        row_count = low.shape[0]
        qkv_own = jnp.concatenate(
            [low.reshape(row_count, 3, half_width), high.reshape(row_count, 3, half_width)], axis=2
        ).transpose(1, 0, 2)
        return (
            qkv_own,
            jnp.concatenate(join_cores(found[-3], 1), axis=0),
            jnp.concatenate(join_cores(found[-2], 0), axis=1),
            jnp.concatenate(join_cores(found[-1], 1), axis=0),
        )

    weight_grads = [
        own_grads(number) if all(chain.place > steps for chain in reductions[number]) else None
        for number in range(layers)
    ]
    summed = jnp.stack(small_grads)
    upstream, summed, weight_grads = lax.optimization_barrier((upstream, summed, weight_grads))
    grad_input = give_back(upstream.astype(BF16))
    small_masks = [span_masks[bit] for bit in span_bits] + [pair_masks[bit] for bit in pair_bits]
    running = [chain for chain in running if chain.place <= steps]
    while running or small_masks:
        if small_masks:
            passed = swap(summed, small_masks[0])
        passed = advance(passed, running)
        if small_masks:
            summed = summed + passed
            small_masks = small_masks[1:]
        running = [chain for chain in running if chain.place <= steps]
    weight_grads = [
        own_grads(number) if weight_grads[number] is None else weight_grads[number]
        for number in range(layers)
    ]

    row_total = 6 * features
    own = features // devices
    row_summed = lax.dynamic_slice_in_dim(
        summed[:, :row_total].reshape(layers, 6, features),
        (dp_at * tensor_size + tensor_at) * own,
        own,
        2,
    )
    units = summed[:, row_total:].reshape(layers, spans, -1)
    units = lax.dynamic_slice_in_dim(units, span, 1, 1)[:, 0]
    other_units = swap(units, core_mask)
    units = jnp.where(core_one == (dp_at >= pairs), units, other_units)
    place = dp_at % pairs
    qv_part = units[:, : 2 * half_width].reshape(layers, 2, pairs, -1)
    up_part = units[:, 2 * half_width :].reshape(layers, pairs, -1)
    qv_own = lax.dynamic_slice_in_dim(qv_part, place, 1, 2)[:, :, 0]
    up_own = lax.dynamic_slice_in_dim(up_part, place, 1, 1)[:, 0]

    joined = [
        jnp.stack([weight_grads[number][member] for number in range(layers)]) for member in range(4)
    ]
    return (
        output,
        grad_input.astype(F32),
        joined[0],
        qv_own,
        joined[1],
        joined[2],
        up_own,
        joined[3],
        row_summed,
    )


def solution(mesh):
    placed = (
        P(("dp", "tensor"), None),
        P("dp", None),
        P(None, None, "dp", "tensor"),
        P(None, None, ("tensor", "dp")),
        P(None, "tensor", "dp"),
        P(None, "dp", "tensor"),
        P(None, ("tensor", "dp")),
        P(None, "tensor", "dp"),
        P(None, None, ("dp", "tensor")),
        P(("dp", "tensor"), None),
    )
    return jax.shard_map(
        functools.partial(body, mesh.shape["dp"], mesh.shape["tensor"]),
        mesh=mesh,
        in_specs=placed,
        out_specs=(
            P(("dp", "tensor"), None),
            P(("dp", "tensor"), None),
            P(None, None, "dp", "tensor"),
            P(None, None, ("tensor", "dp")),
            P(None, "tensor", "dp"),
            P(None, "dp", "tensor"),
            P(None, ("tensor", "dp")),
            P(None, "tensor", "dp"),
            P(None, None, ("dp", "tensor")),
        ),
        check_vma=False,
    )
```

```python
import functools

import jax
import jax.numpy as jnp
from jax import lax
from jax.experimental import pallas as pl
from jax.experimental.pallas import tpu as pltpu
from jax.sharding import PartitionSpec as P

HEADS = 16
HEAD_DIM = 64
LANES = 128
QBLK = 256

EPSILON = 1e-05
MASKED = -1e30
BOTH = ("dp", "tensor")
F32 = jnp.float32
BF16 = jnp.bfloat16


def dot_nt(left, right):
    return lax.dot_general(left, right, (((1,), (1,)), ((), ())), preferred_element_type=F32)


def dot_nn(left, right):
    return lax.dot_general(left, right, (((1,), (0,)), ((), ())), preferred_element_type=F32)


def dot_tn(left, right):
    return lax.dot_general(left, right, (((0,), (0,)), ((), ())), preferred_element_type=F32)


def fill_places(seg_col, seg_row, places, length):
    for first in range(0, length, QBLK):
        count = first + QBLK
        key_at = lax.broadcasted_iota(jnp.int32, (count, QBLK), 0)
        query_at = first + lax.broadcasted_iota(jnp.int32, (count, QBLK), 1)
        allowed = (key_at <= query_at) & (
            seg_col[0:count, :] == seg_row[:, first : first + QBLK]
        )
        places[0:count, first : first + QBLK] = jnp.where(
            allowed, key_at.astype(F32), MASKED
        )


def head_lanes(values, member):
    lane = lax.broadcasted_iota(jnp.int32, values.shape, 1)
    return jnp.where(lane // HEAD_DIM == member, values, jnp.zeros_like(values))


def forward_kernel(slopes, query_in, key_in, value_in, seg_col, seg_row, mixed, places):
    group = pl.program_id(0)
    length = query_in.shape[0]

    @pl.when(group == 0)
    def _():
        fill_places(seg_col, seg_row, places, length)

    scale = HEAD_DIM**-0.5
    values_t = value_in[...].astype(F32).T.astype(BF16)
    keys = [
        head_lanes(key_in[...].astype(F32), member).astype(BF16)
        for member in range(2)
    ]
    for first in range(0, length, QBLK):
        count = first + QBLK
        queries = (query_in[first:count, :].astype(F32) * scale).astype(BF16)
        parts = []
        for member in range(2):
            slope = slopes[group, member]
            scores = dot_nt(keys[member][0:count, :], queries)
            scores = scores + slope * places[0:count, first:count]
            top = jnp.max(scores, axis=0, keepdims=True)
            lifted = jnp.exp(scores - top)
            total = jnp.sum(lifted, axis=0, keepdims=True)
            rows = values_t[member * HEAD_DIM : (member + 1) * HEAD_DIM, 0:count]
            parts.append(dot_nn(rows, lifted.astype(BF16)) / total)
        mixed[first:count, :] = jnp.concatenate(parts, axis=0).T.astype(BF16)


def backward_kernel(
    slopes,
    query_in,
    key_in,
    value_in,
    upstream,
    seg_col,
    seg_row,
    packed_grad,
    sums,
    places,
    key_grad,
    value_grad,
):
    group = pl.program_id(0)
    length = query_in.shape[0]

    @pl.when(group == 0)
    def _():
        fill_places(seg_col, seg_row, places, length)

    scale = HEAD_DIM**-0.5
    keys_f32 = key_in[...].astype(F32)
    values_f32 = value_in[...].astype(F32)
    keys = [head_lanes(keys_f32, member).astype(BF16) for member in range(2)]
    value_rows = [head_lanes(values_f32, member).astype(BF16) for member in range(2)]
    keys_t = (keys_f32 * scale).T.astype(BF16)
    query_sum = jnp.zeros((1, LANES), F32)
    for first in reversed(range(0, length, QBLK)):
        count = first + QBLK
        queries_f32 = query_in[first:count, :].astype(F32) * scale
        queries = queries_f32.astype(BF16)
        above_f32 = upstream[first:count, :].astype(F32)
        above = above_f32.astype(BF16)
        parts = []
        key_part = None
        value_part = None
        for member in range(2):
            slope = slopes[group, member]
            scores = dot_nt(keys[member][0:count, :], queries)
            scores = scores + slope * places[0:count, first:count]
            top = jnp.max(scores, axis=0, keepdims=True)
            lifted = jnp.exp(scores - top)
            total = jnp.sum(lifted, axis=0, keepdims=True)
            chances = lifted * (1.0 / total)
            chance_grad = dot_nt(value_rows[member][0:count, :], above)
            inner = jnp.sum(chance_grad * chances, axis=0, keepdims=True)
            score_grad = (chances * (chance_grad - inner)).astype(BF16)
            rows = keys_t[member * HEAD_DIM : (member + 1) * HEAD_DIM, 0:count]
            parts.append(dot_nn(rows, score_grad))
            key_term = dot_nn(score_grad, head_lanes(queries_f32, member).astype(BF16))
            value_term = dot_nn(chances.astype(BF16), head_lanes(above_f32, member).astype(BF16))
            key_part = key_term if member == 0 else key_part + key_term
            value_part = value_term if member == 0 else value_part + value_term
        query_grad = jnp.concatenate(parts, axis=0).T
        query_sum = query_sum + jnp.sum(query_grad, axis=0, keepdims=True)
        packed_grad[0, first:count, :] = query_grad.astype(BF16)
        if count == length:
            key_grad[...] = key_part
            value_grad[...] = value_part
        else:
            key_grad[0:count, :] += key_part
            value_grad[0:count, :] += value_part
    packed_grad[1] = key_grad[...].astype(BF16)
    packed_grad[2] = value_grad[...].astype(BF16)
    sums[0:1, :] = query_sum
    sums[1:2, :] = jnp.sum(value_grad[...], axis=0, keepdims=True)


def column_blocks(packed, length, groups):
    if len(packed) == 1:
        packed = packed * 3
        starts = (0, groups, 2 * groups)
    else:
        starts = (0, 0, 0)
    specs = [
        pl.BlockSpec((length, LANES), functools.partial(lambda start, g: (0, start + g), start))
        for start in starts
    ]
    return packed, specs


def attention_forward(packed, seg_col, seg_row, slopes):
    length = packed[0].shape[0]
    width = sum(array.shape[1] for array in packed) // 3
    groups = width // LANES
    packed, specs = column_blocks(packed, length, groups)
    block = pl.BlockSpec((length, LANES), lambda g: (0, g))
    return pl.pallas_call(
        forward_kernel,
        grid=(groups,),
        in_specs=[
            pl.BlockSpec(memory_space=pltpu.SMEM),
            *specs,
            pl.BlockSpec((length, 1), lambda g: (0, 0)),
            pl.BlockSpec((1, length), lambda g: (0, 0)),
        ],
        out_specs=block,
        out_shape=jax.ShapeDtypeStruct((length, width), BF16),
        scratch_shapes=[pltpu.VMEM((length, length), F32)],
        compiler_params=pltpu.CompilerParams(vmem_limit_bytes=40 * 2**20),
        cost_estimate=pl.CostEstimate(
            flops=groups * 2 * length * length * 256 * 5,
            bytes_accessed=groups * length * LANES * 8,
            transcendentals=groups * length * length * 2,
        ),
    )(slopes, *packed, seg_col, seg_row)


def attention_backward(packed, upstream, seg_col, seg_row, slopes):
    length, width = upstream.shape
    groups = width // LANES
    packed, specs = column_blocks(packed, length, groups)
    block = pl.BlockSpec((length, LANES), lambda g: (0, g))
    return pl.pallas_call(
        backward_kernel,
        grid=(groups,),
        in_specs=[
            pl.BlockSpec(memory_space=pltpu.SMEM),
            *specs,
            block,
            pl.BlockSpec((length, 1), lambda g: (0, 0)),
            pl.BlockSpec((1, length), lambda g: (0, 0)),
        ],
        out_specs=[
            pl.BlockSpec((3, length, LANES), lambda g: (0, 0, g)),
            pl.BlockSpec((None, 2, LANES), lambda g: (g, 0, 0)),
        ],
        out_shape=[
            jax.ShapeDtypeStruct((3, length, width), BF16),
            jax.ShapeDtypeStruct((groups, 2, LANES), F32),
        ],
        scratch_shapes=[
            pltpu.VMEM((length, length), F32),
            pltpu.VMEM((length, LANES), F32),
            pltpu.VMEM((length, LANES), F32),
        ],
        compiler_params=pltpu.CompilerParams(vmem_limit_bytes=48 * 2**20),
        cost_estimate=pl.CostEstimate(
            flops=groups * 2 * length * length * 256 * 8,
            bytes_accessed=groups * length * LANES * 14,
            transcendentals=groups * length * length * 2,
        ),
    )(slopes, *packed, upstream, seg_col, seg_row)


def merge_kernel(axis, first, second, joined):
    size = first.shape[axis]
    for which, source in enumerate((first, second)):
        at = pl.ds(which * size, size)
        if axis == 0:
            joined[at, :] = source[...]
        else:
            joined[:, at] = source[...]


def merge(first, second, size, count, axis):
    shape = list(first.shape)
    shape[axis] *= 2
    grain = LANES if axis == 1 else 16
    if first.size < 2**20 or size % grain or shape[1] % (4 * LANES) or shape[0] % 64:
        parts = []
        for at in range(count):
            for values in (first, second):
                parts.append(lax.slice_in_dim(values, at * size, (at + 1) * size, axis=axis))
        return jnp.concatenate(parts, axis=axis)
    cuts = 4
    if axis == 0:
        block = (size, shape[1] // cuts)
        wide = (2 * size, shape[1] // cuts)
        place = lambda cut, at: (at, cut)
    else:
        block = (shape[0] // cuts, size)
        wide = (shape[0] // cuts, 2 * size)
        place = lambda cut, at: (cut, at)
    return pl.pallas_call(
        functools.partial(merge_kernel, axis),
        grid=(cuts, count),
        in_specs=[pl.BlockSpec(block, place)] * 2,
        out_specs=pl.BlockSpec(wide, place),
        out_shape=jax.ShapeDtypeStruct(tuple(shape), first.dtype),
        compiler_params=pltpu.CompilerParams(vmem_limit_bytes=24 * 2**20),
        cost_estimate=pl.CostEstimate(
            flops=0, bytes_accessed=8 * first.size, transcendentals=0
        ),
    )(first, second)


def normalise(values):
    centred = values - jnp.mean(values, axis=-1, keepdims=True)
    spread = jnp.mean(centred * centred, axis=-1, keepdims=True)
    inverse = lax.rsqrt(spread + EPSILON)
    return centred * inverse, inverse


def layer_norm(values, gain_row, shift_row):
    return normalise(values)[0] * gain_row + shift_row


def norm_back(values, gain_row, upstream):
    unit, inverse = normalise(values)
    gain_grad = jnp.sum(upstream * unit, axis=0)
    shift_grad = jnp.sum(upstream, axis=0)
    inner = upstream * gain_row
    result = inverse * (
        inner
        - jnp.mean(inner, axis=-1, keepdims=True)
        - unit * jnp.mean(inner * unit, axis=-1, keepdims=True)
    )
    return result, gain_grad, shift_grad


def gelu_tanh(values):
    return jax.nn.gelu(values, approximate=True)


def bits_of(count):
    return [1 << place for place in range(count.bit_length() - 1)]


def body(
    dp_size,
    tensor_size,
    tokens_in,
    segment_ids,
    qkv_weight,
    qv_bias,
    out_weight,
    up_weight,
    up_bias,
    down_weight,
    row_params,
    cotangent,
):
    layers = qkv_weight.shape[0]
    shard_rows, features = tokens_in.shape
    spans = 2 * segment_ids.shape[0]
    inner_size = tensor_size // spans
    pairs = dp_size // 2
    devices = dp_size * tensor_size
    heads_half = HEADS // tensor_size // 2
    half_width = heads_half * HEAD_DIM

    dp_at = lax.axis_index("dp")
    tensor_at = lax.axis_index("tensor")
    core = dp_at % 2
    pair = dp_at // 2
    span = tensor_at // inner_size
    inner = tensor_at % inner_size
    core_one = core == 1

    core_mask = tensor_size
    inner_masks = bits_of(inner_size)
    span_bits = bits_of(spans)
    pair_bits = bits_of(pairs)
    span_masks = {bit: bit * inner_size for bit in span_bits}
    pair_masks = {bit: bit * 2 * tensor_size for bit in pair_bits}

    def swap(values, mask):
        return lax.ppermute(values, BOTH, [(at, at ^ mask) for at in range(devices)])

    def crossed(at):
        at_core = (at // tensor_size) % 2
        at_span = (at % tensor_size) // inner_size
        return at if at_core == at_span % 2 else at ^ (core_mask | inner_size)

    def cross(values):
        moves = [(at, crossed(at)) for at in range(devices) if at != crossed(at)]
        return jnp.where(core == span % 2, values, lax.ppermute(values, BOTH, moves))

    def ordered(values, mask, is_high, axis):
        other = swap(values, mask)
        return jnp.concatenate(
            [jnp.where(is_high, other, values), jnp.where(is_high, values, other)], axis=axis
        )

    def group_rows(values):
        for mask in inner_masks:
            values = ordered(values, mask, (inner & mask) != 0, 0)
        return ordered(values, core_mask, core_one, 0)

    def group_sum(values):
        for mask in inner_masks + [core_mask]:
            low = values.astype(BF16)
            values = low.astype(F32) + swap(low, mask).astype(F32)
        return values

    high_spans = [("span", bit) for bit in reversed(span_bits[1:])]
    turning = [("pair", bit) for bit in pair_bits]
    turning = turning[:1] + [("span", bit) for bit in span_bits[:1]] + turning[1:]
    orders = [high_spans + turning[by:] + turning[:by] for by in range(3)]

    def mask_of(kind, bit):
        return span_masks[bit] if kind == "span" else pair_masks[bit]

    def interleave(kind, bit, present, width, outer=1):
        lower = sum(1 for at_kind, at in present if at_kind == kind and at < bit)
        upper = sum(1 for at_kind, at in present if at_kind == kind and at > bit)
        return width << lower, (outer if kind == "span" else 1) << upper

    def halves_of(values, kind, bit, present, width, axis, outer):
        size, count = interleave(kind, bit, present, width, outer)
        halves = []
        for which in range(2):
            parts = [
                lax.slice_in_dim(
                    values, (2 * at + which) * size, (2 * at + which + 1) * size, axis=axis
                )
                for at in range(count)
            ]
            halves.append(parts[0] if count == 1 else jnp.concatenate(parts, axis=axis))
        return halves

    class Fetch:
        def __init__(self, block, feature_axis, order, outer=1):
            self.block = block
            self.outer = outer
            self.feature_axis = feature_axis
            self.order = orders[order]
            self.widths = {
                "pair": block.shape[feature_axis],
                "span": block.shape[1 - feature_axis] // outer,
            }
            self.place = 0

        def send(self):
            self.other = swap(self.block, mask_of(*self.order[self.place]))

        def take(self):
            kind, bit = self.order[self.place]
            axis = self.feature_axis if kind == "pair" else 1 - self.feature_axis
            present = self.order[: self.place]
            size, count = interleave(kind, bit, present, self.widths[kind], self.outer)
            self.block = merge(self.block, self.other, size, count, axis)
            self.place += 1
            if self.place < len(self.order):
                self.send()

    class Reduce:
        def __init__(self, feature_side, unit_side, feature_axis, order, outer=1):
            self.feature_axis = feature_axis
            self.outer = outer
            self.order = list(reversed(orders[order]))
            self.widths = {
                "pair": feature_side.shape[1] // pairs,
                "span": unit_side.shape[1] // spans // outer,
            }
            kind, bit = self.order[0]
            sides = {"pair": feature_side, "span": unit_side}
            found = []
            for part in halves_of(
                sides[kind], kind, bit, self.order[1:], self.widths[kind], 1, outer
            ):
                sides[kind] = part
                pair_of = [sides["pair"], sides["span"]]
                if feature_axis == 1:
                    pair_of.reverse()
                found.append(dot_tn(*pair_of).astype(BF16))
            self.keep, send = found
            self.other = swap(send, mask_of(kind, bit))
            self.place = 1

        def take(self):
            ours = self.keep
            theirs = self.other
            if self.place == len(self.order):
                self.result = ours.astype(F32) + theirs.astype(F32)
                self.place += 1
                return
            kind, bit = self.order[self.place]
            axis = self.feature_axis if kind == "pair" else 1 - self.feature_axis
            rest = self.order[self.place + 1 :]
            width = self.widths[kind]
            sums = [
                (first.astype(F32) + second.astype(F32)).astype(BF16)
                for first, second in zip(
                    halves_of(ours, kind, bit, rest, width, axis, self.outer),
                    halves_of(theirs, kind, bit, rest, width, axis, self.outer),
                )
            ]
            self.keep = sums[0]
            self.other = swap(sums[1], mask_of(kind, bit))
            self.place += 1

    def advance(values, chains):
        return tick(values, [chain for chain in chains if chain.place <= steps])

    def tick(values, chains):
        if not chains:
            return values
        values, others = lax.optimization_barrier((values, [chain.other for chain in chains]))
        for chain, other in zip(chains, others):
            chain.other = other
            chain.take()
        return values

    def to_local(values):
        axis = values.ndim - 1
        wide = features // pairs
        return jnp.concatenate(
            [
                lax.dynamic_slice_in_dim(values, (pair ^ offset) * wide, wide, axis)
                for offset in range(pairs)
            ],
            axis=axis,
        )

    from_local = to_local

    def split_cores(low, high, axis):
        mine = jnp.where(core_one, high, low)
        other = swap(jnp.where(core_one, low, high), core_mask)
        return jnp.concatenate(
            [jnp.where(core_one, other, mine), jnp.where(core_one, mine, other)], axis=axis
        )

    def blocks_of(number, which):
        if which == 0:
            local = qkv_weight[number].transpose(1, 0, 2)
            rows = local.shape[0]
            low = local[:, :, :half_width].reshape(rows, 3 * half_width)
            high = local[:, :, half_width:].reshape(rows, 3 * half_width)
            qkv = split_cores(low, high, 0)
            if number:
                found = [(qkv, 0, 2, 3)]
            else:
                found = [
                    (qkv[:, at * half_width : (at + 1) * half_width], 0, at, 1) for at in range(3)
                ]
            half = out_weight.shape[1] // 2
            out = split_cores(out_weight[number, :half], out_weight[number, half:], 1)
            return found + [(out, 1, 2, 1)]
        half = up_weight.shape[2] // 2
        up = split_cores(up_weight[number, :, :half], up_weight[number, :, half:], 0)
        half = down_weight.shape[1] // 2
        down = split_cores(down_weight[number, :half], down_weight[number, half:], 1)
        return [(up, 0, 0, 1), (down, 1, 1, 1)]

    def join_cores(values, feature_axis):
        size = values.shape[feature_axis] // 2
        first = lax.slice_in_dim(values, 0, size, axis=feature_axis)
        second = lax.slice_in_dim(values, size, 2 * size, axis=feature_axis)
        mine = jnp.where(core_one, second, first)
        other = swap(jnp.where(core_one, first, second).astype(BF16), core_mask).astype(F32)
        return jnp.where(core_one, other, mine), jnp.where(core_one, mine, other)

    steps = len(orders[0])

    def fetches_of(blocks):
        return [Fetch(block, axis, order, outer) for block, axis, order, outer in blocks]

    early = fetches_of(blocks_of(0, 0))
    for chain in early:
        chain.send()
    others, rest = lax.optimization_barrier(
        (
            [chain.other for chain in early],
            (tokens_in, segment_ids, out_weight, qkv_weight, up_weight, down_weight),
        )
    )
    for chain, other in zip(early, others):
        chain.other = other
    tokens_in, segment_ids, out_weight, qkv_weight, up_weight, down_weight = rest
    small = jnp.concatenate(
        [row_params.reshape(-1), qv_bias.reshape(-1), up_bias.reshape(-1)]
    )[None]

    def small_hop(values, mask):
        return ordered(values, mask, (dp_at * tensor_size + tensor_at) & mask != 0, 0)

    small_hops = bits_of(devices)
    small = small_hop(small, small_hops[0])
    small = tick(small, early)
    tokens_here = cross(tokens_in)
    first_stage = fetches_of(blocks_of(0, 1))
    next_fetches = []
    if layers > 1:
        next_fetches = fetches_of(blocks_of(1, 0))
    first_stage = first_stage + next_fetches
    small = small_hop(small, small_hops[1])
    small, tokens_here, first_blocks = tick(
        (small, tokens_here, [chain.block for chain in first_stage]), early
    )
    for chain, block in zip(first_stage, first_blocks):
        chain.block = block
        chain.send()
    stream = group_rows(tokens_here)
    small = small_hop(small, small_hops[2])
    small, stream = tick((small, stream), early)
    stream = to_local(stream).astype(F32)
    for mask in small_hops[3:]:
        small = small_hop(small, mask)
    later_others, small = tick(([chain.other for chain in first_stage], small), early)
    for chain, other in zip(first_stage, later_others):
        chain.other = other
    while early[0].place < steps:
        for chain in early:
            chain.take()

    row_size, qv_size = row_params.size, qv_bias.size
    rows_every = to_local(
        small[:, :row_size]
        .reshape(devices, layers, 6, -1)
        .transpose(1, 2, 0, 3)
        .reshape(layers, 6, features)
        .astype(F32)
    )

    def local_units(values, kinds):
        values = values.reshape(dp_size, spans, inner_size, layers, kinds, -1)
        values = lax.dynamic_slice_in_dim(values, core * pairs, pairs, 0)
        values = lax.dynamic_slice_in_dim(values, inner, 1, 2)[:, :, 0]
        blocks = [
            lax.dynamic_slice_in_dim(values, span ^ offset, 1, 1)[:, 0] for offset in range(spans)
        ]
        values = jnp.stack(blocks)
        return values.transpose(2, 3, 0, 1, 4).reshape(layers, kinds, -1).astype(F32)

    qv_local = local_units(small[:, row_size : row_size + qv_size], 2)
    up_bias_local = local_units(small[:, row_size + qv_size :], 1)[:, 0]

    span_at = jnp.stack([span ^ offset for offset in range(spans)])
    heads_at = (span_at * inner_size + inner)[:, None] * (2 * heads_half) + core * heads_half
    heads_at = heads_at + jnp.arange(heads_half, dtype=jnp.int32)[None]
    slopes = (2.0 ** (-8.0 * (heads_at.astype(F32) + 1.0) / HEADS)).reshape(-1, 2)

    own_segment = lax.dynamic_slice_in_dim(segment_ids, span // 2, 1, 0)
    seg_row = jnp.where(core == span % 2, own_segment, swap(own_segment, core_mask))
    seg_col = seg_row.reshape(-1, 1)

    fetches = [early + first_stage[:2], first_stage[2:]]
    stages = [early, first_stage]
    for number in range(1, layers):
        late = fetches_of(blocks_of(number, 1))
        fetches[number] = fetches[number] + late
        if number + 1 < layers:
            fetches.append(fetches_of(blocks_of(number + 1, 0)))
            late = late + fetches[number + 1]
        stages.append(late)
    for before, after in zip(stages[1:-1], stages[2:]):
        held = lax.optimization_barrier(
            ([chain.other for chain in before], [chain.block for chain in after])
        )
        for chain, other in zip(before, held[0]):
            chain.other = other
        for chain, block in zip(after, held[1]):
            chain.block = block
            chain.send()

    stash = []
    normed = layer_norm(stream, rows_every[0, 0], rows_every[0, 1]).astype(BF16)
    for number in range(layers):
        rows = rows_every[number]
        stage = stages[number + 1]
        weights = [chain.block for chain in fetches[number]]
        weights = weights[: len(weights) - 2] + [None, None]
        biases = (qv_local[number, 0], jnp.zeros_like(qv_local[number, 0]), qv_local[number, 1])
        if number:
            biases = (jnp.concatenate(biases),)
        packed = [
            (jnp.dot(normed, weight, preferred_element_type=F32) + bias).astype(BF16)
            for weight, bias in zip(weights[:-3], biases)
        ]
        if number == 0:
            packed = tick(packed, stage)
            packed, cotangent = lax.optimization_barrier((packed, cotangent))
            upstream_low = to_local(group_rows(cross(cotangent)))
        attended = attention_forward(packed, seg_col, seg_row, slopes)
        if number == 0:
            attended = tick(attended, stage)
        middle = stream + (
            group_sum(jnp.dot(attended, weights[-3], preferred_element_type=F32)) + rows[2]
        )
        normed_two = layer_norm(middle, rows[3], rows[4]).astype(BF16)
        while stage[0].place + 1 < steps:
            normed_two = tick(normed_two, stage)
        following = stages[number + 2] if number + 2 < len(stages) else []
        if following:
            normed_two = tick(normed_two, stage)
            weights_two, others = lax.optimization_barrier(
                ([chain.block for chain in stage], [chain.other for chain in following])
            )
            for chain, block in zip(stage, weights_two):
                chain.block = block
            for chain, other in zip(following, others):
                chain.other = other
                chain.take()
        else:
            for chain in stage:
                chain.take()
        weights = [chain.block for chain in fetches[number]]
        pre_gelu = (
            jnp.dot(normed_two, weights[-2], preferred_element_type=F32) + up_bias_local[number]
        )
        hidden = gelu_tanh(pre_gelu).astype(BF16)
        if following:
            hidden = tick(hidden, following)
        stash.append(
            (stream, normed, packed, attended, middle, normed_two, pre_gelu, hidden, weights)
        )
        stream = middle + (
            group_sum(jnp.dot(hidden, weights[-1], preferred_element_type=F32)) + rows[5]
        )
        if number + 1 < layers:
            after = rows_every[number + 1]
            normed = layer_norm(stream, after[0], after[1]).astype(BF16)
            if following[0].place + 1 < steps:
                normed = tick(normed, following)

    def give_back(values):
        at = (core * inner_size + inner) * shard_rows
        return cross(lax.dynamic_slice_in_dim(from_local(values), at, shard_rows, 0))

    output = give_back(stream.astype(BF16))

    upstream = upstream_low.astype(F32)
    reductions = [None] * layers
    small_grads = [None] * layers
    running = []
    for number in reversed(range(layers)):
        (
            stream_in,
            normed,
            packed,
            attended,
            middle,
            normed_two,
            pre_gelu,
            hidden,
            weights,
        ) = stash[number]
        rows = rows_every[number]
        apart = len(packed) == 3

        down_bias_grad = jnp.sum(upstream, axis=0)
        down_in = upstream.astype(BF16)
        down_chain = Reduce(down_in, hidden, 1, 1)
        hidden_grad = dot_nt(down_in, weights[-1])
        pre_grad = jax.vjp(gelu_tanh, pre_gelu)[1](hidden_grad)[0]
        up_bias_grad = jnp.sum(pre_grad, axis=0)
        pre_low = pre_grad.astype(BF16)
        pre_low = advance(pre_low, running)
        up_chain = Reduce(normed_two, pre_low, 0, 0)
        normed_two_grad = group_sum(dot_nt(pre_low, weights[-2]))
        middle_grad, gain_two_grad, shift_two_grad = norm_back(middle, rows[3], normed_two_grad)
        middle_grad = middle_grad + upstream
        out_bias_grad = jnp.sum(middle_grad, axis=0)
        out_in = middle_grad.astype(BF16)
        attended_grad = dot_nt(out_in, weights[-3]).astype(BF16)
        attended_grad = advance(attended_grad, running if number else running + [down_chain])
        out_chain = Reduce(out_in, attended, 1, 2)
        packed_grad, qv_sums = attention_backward(packed, attended_grad, seg_col, seg_row, slopes)
        packed_grad = advance(packed_grad, running + [down_chain, up_chain, out_chain])
        if apart:
            qkv_chains = [Reduce(normed, packed_grad[at], 0, at) for at in range(3)]
            normed_grad = (
                dot_nt(packed_grad[0], weights[0])
                + dot_nt(packed_grad[1], weights[1])
                + dot_nt(packed_grad[2], weights[2])
            )
        else:
            beside = jnp.concatenate([packed_grad[at] for at in range(3)], axis=1)
            qkv_chains = [Reduce(normed, beside, 0, 2, 3)]
            normed_grad = dot_nt(beside, weights[0])
        normed_grad = group_sum(normed_grad)
        stream_grad, gain_one_grad, shift_one_grad = norm_back(stream_in, rows[0], normed_grad)
        upstream = middle_grad + stream_grad
        if number:
            upstream = advance(upstream, running + [down_chain, up_chain, out_chain])
        running = running + [down_chain, up_chain, out_chain] + qkv_chains
        reductions[number] = qkv_chains + [out_chain, up_chain, down_chain]

        row_grads = from_local(
            jnp.stack(
                [
                    gain_one_grad,
                    shift_one_grad,
                    out_bias_grad,
                    gain_two_grad,
                    shift_two_grad,
                    down_bias_grad,
                ]
            )
        )
        qv_units = qv_sums.transpose(1, 0, 2).reshape(2, spans, half_width)
        units = jnp.concatenate(
            [qv_units.transpose(1, 0, 2).reshape(spans, -1), up_bias_grad.reshape(spans, -1)],
            axis=1,
        )
        units = jnp.concatenate(
            [
                lax.dynamic_slice_in_dim(units, span ^ true_span, 1, 0)
                for true_span in range(spans)
            ],
            axis=0,
        )
        small_grads[number] = jnp.concatenate([row_grads.reshape(-1), units.reshape(-1)])
    def own_grads(number):
        found = [chain.result for chain in reductions[number]]
        low, high = join_cores(jnp.concatenate(found[:-3], axis=1), 0)
        row_count = low.shape[0]
        qkv_own = jnp.concatenate(
            [low.reshape(row_count, 3, half_width), high.reshape(row_count, 3, half_width)], axis=2
        ).transpose(1, 0, 2)
        return (
            qkv_own,
            jnp.concatenate(join_cores(found[-3], 1), axis=0),
            jnp.concatenate(join_cores(found[-2], 0), axis=1),
            jnp.concatenate(join_cores(found[-1], 1), axis=0),
        )

    upstream = advance(upstream, [chain for chains in reductions[1:] for chain in chains])
    weight_grads = [
        own_grads(number) if all(chain.place > steps for chain in reductions[number]) else None
        for number in range(layers)
    ]
    summed = jnp.stack(small_grads)
    upstream, summed, weight_grads = lax.optimization_barrier((upstream, summed, weight_grads))
    grad_input = give_back(upstream.astype(BF16))
    small_masks = [span_masks[bit] for bit in span_bits] + [pair_masks[bit] for bit in pair_bits]
    running = [chain for chain in running if chain.place <= steps]
    while running or small_masks:
        if small_masks:
            passed = swap(summed, small_masks[0])
        passed = advance(passed, running)
        if small_masks:
            summed = summed + passed
            small_masks = small_masks[1:]
        running = [chain for chain in running if chain.place <= steps]
    weight_grads = [
        own_grads(number) if weight_grads[number] is None else weight_grads[number]
        for number in range(layers)
    ]

    row_total = 6 * features
    own = features // devices
    row_summed = lax.dynamic_slice_in_dim(
        summed[:, :row_total].reshape(layers, 6, features),
        (dp_at * tensor_size + tensor_at) * own,
        own,
        2,
    )
    units = summed[:, row_total:].reshape(layers, spans, -1)
    units = lax.dynamic_slice_in_dim(units, span, 1, 1)[:, 0]
    other_units = swap(units, core_mask)
    units = jnp.where(core_one == (dp_at >= pairs), units, other_units)
    place = dp_at % pairs
    qv_part = units[:, : 2 * half_width].reshape(layers, 2, pairs, -1)
    up_part = units[:, 2 * half_width :].reshape(layers, pairs, -1)
    qv_own = lax.dynamic_slice_in_dim(qv_part, place, 1, 2)[:, :, 0]
    up_own = lax.dynamic_slice_in_dim(up_part, place, 1, 1)[:, 0]

    joined = [
        jnp.stack([weight_grads[number][member] for number in range(layers)]) for member in range(4)
    ]
    return (
        output,
        grad_input.astype(F32),
        joined[0],
        qv_own,
        joined[1],
        joined[2],
        up_own,
        joined[3],
        row_summed,
    )


def solution(mesh):
    placed = (
        P(("dp", "tensor"), None),
        P("dp", None),
        P(None, None, "dp", "tensor"),
        P(None, None, ("tensor", "dp")),
        P(None, "tensor", "dp"),
        P(None, "dp", "tensor"),
        P(None, ("tensor", "dp")),
        P(None, "tensor", "dp"),
        P(None, None, ("dp", "tensor")),
        P(("dp", "tensor"), None),
    )
    return jax.shard_map(
        functools.partial(body, mesh.shape["dp"], mesh.shape["tensor"]),
        mesh=mesh,
        in_specs=placed,
        out_specs=(
            P(("dp", "tensor"), None),
            P(("dp", "tensor"), None),
            P(None, None, "dp", "tensor"),
            P(None, None, ("tensor", "dp")),
            P(None, "tensor", "dp"),
            P(None, "dp", "tensor"),
            P(None, ("tensor", "dp")),
            P(None, "tensor", "dp"),
            P(None, None, ("dp", "tensor")),
        ),
        check_vma=False,
    )
```

```python
import functools

import jax
import jax.numpy as jnp
from jax import lax
from jax.experimental import pallas as pl
from jax.experimental.pallas import tpu as pltpu
from jax.sharding import PartitionSpec as P

HEADS = 16
HEAD_DIM = 64
LANES = 128
QBLK = 256

EPSILON = 1e-05
MASKED = -1e30
BOTH = ("dp", "tensor")
F32 = jnp.float32
BF16 = jnp.bfloat16


def dot_nt(left, right):
    return lax.dot_general(left, right, (((1,), (1,)), ((), ())), preferred_element_type=F32)


def dot_nn(left, right):
    return lax.dot_general(left, right, (((1,), (0,)), ((), ())), preferred_element_type=F32)


def dot_tn(left, right):
    return lax.dot_general(left, right, (((0,), (0,)), ((), ())), preferred_element_type=F32)


def fill_places(seg_col, seg_row, places, length):
    for first in range(0, length, QBLK):
        count = first + QBLK
        key_at = lax.broadcasted_iota(jnp.int32, (count, QBLK), 0)
        query_at = first + lax.broadcasted_iota(jnp.int32, (count, QBLK), 1)
        allowed = (key_at <= query_at) & (
            seg_col[0:count, :] == seg_row[:, first : first + QBLK]
        )
        places[0:count, first : first + QBLK] = jnp.where(
            allowed, key_at.astype(F32), MASKED
        )


def head_lanes(values, member):
    lane = lax.broadcasted_iota(jnp.int32, values.shape, 1)
    return jnp.where(lane // HEAD_DIM == member, values, jnp.zeros_like(values))


def forward_kernel(slopes, query_in, key_in, value_in, seg_col, seg_row, mixed, places):
    group = pl.program_id(0)
    length = query_in.shape[0]

    @pl.when(group == 0)
    def _():
        fill_places(seg_col, seg_row, places, length)

    scale = HEAD_DIM**-0.5
    values_t = value_in[...].astype(F32).T.astype(BF16)
    keys = [
        head_lanes(key_in[...].astype(F32), member).astype(BF16)
        for member in range(2)
    ]
    for first in range(0, length, QBLK):
        count = first + QBLK
        queries = (query_in[first:count, :].astype(F32) * scale).astype(BF16)
        parts = []
        for member in range(2):
            slope = slopes[group, member]
            scores = dot_nt(keys[member][0:count, :], queries)
            scores = scores + slope * places[0:count, first:count]
            top = jnp.max(scores, axis=0, keepdims=True)
            lifted = jnp.exp(scores - top)
            total = jnp.sum(lifted, axis=0, keepdims=True)
            rows = values_t[member * HEAD_DIM : (member + 1) * HEAD_DIM, 0:count]
            parts.append(dot_nn(rows, lifted.astype(BF16)) / total)
        mixed[first:count, :] = jnp.concatenate(parts, axis=0).T.astype(BF16)


def backward_kernel(
    slopes,
    query_in,
    key_in,
    value_in,
    upstream,
    seg_col,
    seg_row,
    packed_grad,
    sums,
    places,
    key_grad,
    value_grad,
):
    group = pl.program_id(0)
    length = query_in.shape[0]

    @pl.when(group == 0)
    def _():
        fill_places(seg_col, seg_row, places, length)

    scale = HEAD_DIM**-0.5
    keys_f32 = key_in[...].astype(F32)
    values_f32 = value_in[...].astype(F32)
    keys = [head_lanes(keys_f32, member).astype(BF16) for member in range(2)]
    value_rows = [head_lanes(values_f32, member).astype(BF16) for member in range(2)]
    keys_t = (keys_f32 * scale).T.astype(BF16)
    query_sum = jnp.zeros((1, LANES), F32)
    for first in reversed(range(0, length, QBLK)):
        count = first + QBLK
        queries_f32 = query_in[first:count, :].astype(F32) * scale
        queries = queries_f32.astype(BF16)
        above_f32 = upstream[first:count, :].astype(F32)
        above = above_f32.astype(BF16)
        parts = []
        key_part = None
        value_part = None
        for member in range(2):
            slope = slopes[group, member]
            scores = dot_nt(keys[member][0:count, :], queries)
            scores = scores + slope * places[0:count, first:count]
            top = jnp.max(scores, axis=0, keepdims=True)
            lifted = jnp.exp(scores - top)
            total = jnp.sum(lifted, axis=0, keepdims=True)
            chances = lifted * (1.0 / total)
            chance_grad = dot_nt(value_rows[member][0:count, :], above)
            inner = jnp.sum(chance_grad * chances, axis=0, keepdims=True)
            score_grad = (chances * (chance_grad - inner)).astype(BF16)
            rows = keys_t[member * HEAD_DIM : (member + 1) * HEAD_DIM, 0:count]
            parts.append(dot_nn(rows, score_grad))
            key_term = dot_nn(score_grad, head_lanes(queries_f32, member).astype(BF16))
            value_term = dot_nn(chances.astype(BF16), head_lanes(above_f32, member).astype(BF16))
            key_part = key_term if member == 0 else key_part + key_term
            value_part = value_term if member == 0 else value_part + value_term
        query_grad = jnp.concatenate(parts, axis=0).T
        query_sum = query_sum + jnp.sum(query_grad, axis=0, keepdims=True)
        packed_grad[0, first:count, :] = query_grad.astype(BF16)
        if count == length:
            key_grad[...] = key_part
            value_grad[...] = value_part
        else:
            key_grad[0:count, :] += key_part
            value_grad[0:count, :] += value_part
    packed_grad[1] = key_grad[...].astype(BF16)
    packed_grad[2] = value_grad[...].astype(BF16)
    sums[0:1, :] = query_sum
    sums[1:2, :] = jnp.sum(value_grad[...], axis=0, keepdims=True)


def column_blocks(packed, length, groups):
    if len(packed) == 1:
        packed = packed * 3
        starts = (0, groups, 2 * groups)
    else:
        starts = (0, 0, 0)
    specs = [
        pl.BlockSpec((length, LANES), functools.partial(lambda start, g: (0, start + g), start))
        for start in starts
    ]
    return packed, specs


def attention_forward(packed, seg_col, seg_row, slopes):
    length = packed[0].shape[0]
    width = sum(array.shape[1] for array in packed) // 3
    groups = width // LANES
    packed, specs = column_blocks(packed, length, groups)
    block = pl.BlockSpec((length, LANES), lambda g: (0, g))
    return pl.pallas_call(
        forward_kernel,
        grid=(groups,),
        in_specs=[
            pl.BlockSpec(memory_space=pltpu.SMEM),
            *specs,
            pl.BlockSpec((length, 1), lambda g: (0, 0)),
            pl.BlockSpec((1, length), lambda g: (0, 0)),
        ],
        out_specs=block,
        out_shape=jax.ShapeDtypeStruct((length, width), BF16),
        scratch_shapes=[pltpu.VMEM((length, length), F32)],
        compiler_params=pltpu.CompilerParams(vmem_limit_bytes=40 * 2**20),
        cost_estimate=pl.CostEstimate(
            flops=groups * 2 * length * length * 256 * 5,
            bytes_accessed=groups * length * LANES * 8,
            transcendentals=groups * length * length * 2,
        ),
    )(slopes, *packed, seg_col, seg_row)


def attention_backward(packed, upstream, seg_col, seg_row, slopes):
    length, width = upstream.shape
    groups = width // LANES
    packed, specs = column_blocks(packed, length, groups)
    block = pl.BlockSpec((length, LANES), lambda g: (0, g))
    return pl.pallas_call(
        backward_kernel,
        grid=(groups,),
        in_specs=[
            pl.BlockSpec(memory_space=pltpu.SMEM),
            *specs,
            block,
            pl.BlockSpec((length, 1), lambda g: (0, 0)),
            pl.BlockSpec((1, length), lambda g: (0, 0)),
        ],
        out_specs=[
            pl.BlockSpec((3, length, LANES), lambda g: (0, 0, g)),
            pl.BlockSpec((None, 2, LANES), lambda g: (g, 0, 0)),
        ],
        out_shape=[
            jax.ShapeDtypeStruct((3, length, width), BF16),
            jax.ShapeDtypeStruct((groups, 2, LANES), F32),
        ],
        scratch_shapes=[
            pltpu.VMEM((length, length), F32),
            pltpu.VMEM((length, LANES), F32),
            pltpu.VMEM((length, LANES), F32),
        ],
        compiler_params=pltpu.CompilerParams(vmem_limit_bytes=48 * 2**20),
        cost_estimate=pl.CostEstimate(
            flops=groups * 2 * length * length * 256 * 8,
            bytes_accessed=groups * length * LANES * 14,
            transcendentals=groups * length * length * 2,
        ),
    )(slopes, *packed, upstream, seg_col, seg_row)


def merge_kernel(axis, first, second, joined):
    size = first.shape[axis]
    for which, source in enumerate((first, second)):
        at = pl.ds(which * size, size)
        if axis == 0:
            joined[at, :] = source[...]
        else:
            joined[:, at] = source[...]


def merge(first, second, size, count, axis):
    shape = list(first.shape)
    shape[axis] *= 2
    grain = LANES if axis == 1 else 16
    if first.size < 2**20 or size % grain or shape[1] % (4 * LANES) or shape[0] % 64:
        parts = []
        for at in range(count):
            for values in (first, second):
                parts.append(lax.slice_in_dim(values, at * size, (at + 1) * size, axis=axis))
        return jnp.concatenate(parts, axis=axis)
    cuts = 4
    if axis == 0:
        block = (size, shape[1] // cuts)
        wide = (2 * size, shape[1] // cuts)
        place = lambda cut, at: (at, cut)
    else:
        block = (shape[0] // cuts, size)
        wide = (shape[0] // cuts, 2 * size)
        place = lambda cut, at: (cut, at)
    return pl.pallas_call(
        functools.partial(merge_kernel, axis),
        grid=(cuts, count),
        in_specs=[pl.BlockSpec(block, place)] * 2,
        out_specs=pl.BlockSpec(wide, place),
        out_shape=jax.ShapeDtypeStruct(tuple(shape), first.dtype),
        compiler_params=pltpu.CompilerParams(vmem_limit_bytes=24 * 2**20),
        cost_estimate=pl.CostEstimate(
            flops=0, bytes_accessed=8 * first.size, transcendentals=0
        ),
    )(first, second)


def normalise(values):
    centred = values - jnp.mean(values, axis=-1, keepdims=True)
    spread = jnp.mean(centred * centred, axis=-1, keepdims=True)
    inverse = lax.rsqrt(spread + EPSILON)
    return centred * inverse, inverse


def layer_norm(values, gain_row, shift_row):
    return normalise(values)[0] * gain_row + shift_row


def norm_back(values, gain_row, upstream):
    unit, inverse = normalise(values)
    gain_grad = jnp.sum(upstream * unit, axis=0)
    shift_grad = jnp.sum(upstream, axis=0)
    inner = upstream * gain_row
    result = inverse * (
        inner
        - jnp.mean(inner, axis=-1, keepdims=True)
        - unit * jnp.mean(inner * unit, axis=-1, keepdims=True)
    )
    return result, gain_grad, shift_grad


def gelu_tanh(values):
    return jax.nn.gelu(values, approximate=True)


def bits_of(count):
    return [1 << place for place in range(count.bit_length() - 1)]


def body(
    dp_size,
    tensor_size,
    tokens_in,
    segment_ids,
    qkv_weight,
    qv_bias,
    out_weight,
    up_weight,
    up_bias,
    down_weight,
    row_params,
    cotangent,
):
    layers = qkv_weight.shape[0]
    shard_rows, features = tokens_in.shape
    spans = 2 * segment_ids.shape[0]
    inner_size = tensor_size // spans
    pairs = dp_size // 2
    devices = dp_size * tensor_size
    heads_half = HEADS // tensor_size // 2
    half_width = heads_half * HEAD_DIM

    dp_at = lax.axis_index("dp")
    tensor_at = lax.axis_index("tensor")
    core = dp_at % 2
    pair = dp_at // 2
    span = tensor_at // inner_size
    inner = tensor_at % inner_size
    core_one = core == 1

    core_mask = tensor_size
    inner_masks = bits_of(inner_size)
    span_bits = bits_of(spans)
    pair_bits = bits_of(pairs)
    span_masks = {bit: bit * inner_size for bit in span_bits}
    pair_masks = {bit: bit * 2 * tensor_size for bit in pair_bits}

    def swap(values, mask):
        return lax.ppermute(values, BOTH, [(at, at ^ mask) for at in range(devices)])

    def crossed(at):
        at_core = (at // tensor_size) % 2
        at_span = (at % tensor_size) // inner_size
        return at if at_core == at_span % 2 else at ^ (core_mask | inner_size)

    def cross(values):
        moves = [(at, crossed(at)) for at in range(devices) if at != crossed(at)]
        return jnp.where(core == span % 2, values, lax.ppermute(values, BOTH, moves))

    def ordered(values, mask, is_high, axis):
        other = swap(values, mask)
        return jnp.concatenate(
            [jnp.where(is_high, other, values), jnp.where(is_high, values, other)], axis=axis
        )

    def group_rows(values):
        for mask in inner_masks:
            values = ordered(values, mask, (inner & mask) != 0, 0)
        return ordered(values, core_mask, core_one, 0)

    def group_sum(values):
        for mask in inner_masks + [core_mask]:
            low = values.astype(BF16)
            values = low.astype(F32) + swap(low, mask).astype(F32)
        return values

    high_spans = [("span", bit) for bit in reversed(span_bits[1:])]
    turning = [("pair", bit) for bit in pair_bits]
    turning = turning[:1] + [("span", bit) for bit in span_bits[:1]] + turning[1:]
    orders = [high_spans + turning[by:] + turning[:by] for by in range(3)]

    def mask_of(kind, bit):
        return span_masks[bit] if kind == "span" else pair_masks[bit]

    def interleave(kind, bit, present, width, outer=1):
        lower = sum(1 for at_kind, at in present if at_kind == kind and at < bit)
        upper = sum(1 for at_kind, at in present if at_kind == kind and at > bit)
        return width << lower, (outer if kind == "span" else 1) << upper

    def halves_of(values, kind, bit, present, width, axis, outer):
        size, count = interleave(kind, bit, present, width, outer)
        halves = []
        for which in range(2):
            parts = [
                lax.slice_in_dim(
                    values, (2 * at + which) * size, (2 * at + which + 1) * size, axis=axis
                )
                for at in range(count)
            ]
            halves.append(parts[0] if count == 1 else jnp.concatenate(parts, axis=axis))
        return halves

    class Fetch:
        def __init__(self, block, feature_axis, order, outer=1):
            self.block = block
            self.outer = outer
            self.feature_axis = feature_axis
            self.order = orders[order]
            self.widths = {
                "pair": block.shape[feature_axis],
                "span": block.shape[1 - feature_axis] // outer,
            }
            self.place = 0

        def send(self):
            self.other = swap(self.block, mask_of(*self.order[self.place]))

        def take(self):
            kind, bit = self.order[self.place]
            axis = self.feature_axis if kind == "pair" else 1 - self.feature_axis
            present = self.order[: self.place]
            size, count = interleave(kind, bit, present, self.widths[kind], self.outer)
            self.block = merge(self.block, self.other, size, count, axis)
            self.place += 1
            if self.place < len(self.order):
                self.send()

    class Reduce:
        def __init__(self, feature_side, unit_side, feature_axis, order, outer=1):
            self.feature_axis = feature_axis
            self.outer = outer
            self.order = list(reversed(orders[order]))
            self.widths = {
                "pair": feature_side.shape[1] // pairs,
                "span": unit_side.shape[1] // spans // outer,
            }
            kind, bit = self.order[0]
            sides = {"pair": feature_side, "span": unit_side}
            found = []
            for part in halves_of(
                sides[kind], kind, bit, self.order[1:], self.widths[kind], 1, outer
            ):
                sides[kind] = part
                pair_of = [sides["pair"], sides["span"]]
                if feature_axis == 1:
                    pair_of.reverse()
                found.append(dot_tn(*pair_of).astype(BF16))
            self.keep, send = found
            self.other = swap(send, mask_of(kind, bit))
            self.place = 1

        def take(self):
            ours = self.keep
            theirs = self.other
            if self.place == len(self.order):
                self.result = ours.astype(F32) + theirs.astype(F32)
                self.place += 1
                return
            kind, bit = self.order[self.place]
            axis = self.feature_axis if kind == "pair" else 1 - self.feature_axis
            rest = self.order[self.place + 1 :]
            width = self.widths[kind]
            sums = [
                (first.astype(F32) + second.astype(F32)).astype(BF16)
                for first, second in zip(
                    halves_of(ours, kind, bit, rest, width, axis, self.outer),
                    halves_of(theirs, kind, bit, rest, width, axis, self.outer),
                )
            ]
            self.keep = sums[0]
            self.other = swap(sums[1], mask_of(kind, bit))
            self.place += 1

    def advance(values, chains):
        return tick(values, [chain for chain in chains if chain.place <= steps])

    def tick(values, chains):
        if not chains:
            return values
        values, others = lax.optimization_barrier((values, [chain.other for chain in chains]))
        for chain, other in zip(chains, others):
            chain.other = other
            chain.take()
        return values

    def to_local(values):
        axis = values.ndim - 1
        wide = features // pairs
        return jnp.concatenate(
            [
                lax.dynamic_slice_in_dim(values, (pair ^ offset) * wide, wide, axis)
                for offset in range(pairs)
            ],
            axis=axis,
        )

    from_local = to_local

    def split_cores(low, high, axis):
        mine = jnp.where(core_one, high, low)
        other = swap(jnp.where(core_one, low, high), core_mask)
        return jnp.concatenate(
            [jnp.where(core_one, other, mine), jnp.where(core_one, mine, other)], axis=axis
        )

    def blocks_of(number, which):
        if which == 0:
            local = qkv_weight[number].transpose(1, 0, 2)
            rows = local.shape[0]
            low = local[:, :, :half_width].reshape(rows, 3 * half_width)
            high = local[:, :, half_width:].reshape(rows, 3 * half_width)
            qkv = split_cores(low, high, 0)
            if number:
                found = [(qkv, 0, 2, 3)]
            else:
                found = [
                    (qkv[:, at * half_width : (at + 1) * half_width], 0, at, 1) for at in range(3)
                ]
            half = out_weight.shape[1] // 2
            out = split_cores(out_weight[number, :half], out_weight[number, half:], 1)
            return found + [(out, 1, 2, 1)]
        half = up_weight.shape[2] // 2
        up = split_cores(up_weight[number, :, :half], up_weight[number, :, half:], 0)
        half = down_weight.shape[1] // 2
        down = split_cores(down_weight[number, :half], down_weight[number, half:], 1)
        return [(up, 0, 0, 1), (down, 1, 1, 1)]

    def join_cores(values, feature_axis):
        size = values.shape[feature_axis] // 2
        first = lax.slice_in_dim(values, 0, size, axis=feature_axis)
        second = lax.slice_in_dim(values, size, 2 * size, axis=feature_axis)
        mine = jnp.where(core_one, second, first)
        other = swap(jnp.where(core_one, first, second).astype(BF16), core_mask).astype(F32)
        return jnp.where(core_one, other, mine), jnp.where(core_one, mine, other)

    steps = len(orders[0])

    def fetches_of(blocks):
        return [Fetch(block, axis, order, outer) for block, axis, order, outer in blocks]

    early = fetches_of(blocks_of(0, 0))
    for chain in early:
        chain.send()
    others, rest = lax.optimization_barrier(
        (
            [chain.other for chain in early],
            (tokens_in, segment_ids, out_weight, qkv_weight, up_weight, down_weight),
        )
    )
    for chain, other in zip(early, others):
        chain.other = other
    tokens_in, segment_ids, out_weight, qkv_weight, up_weight, down_weight = rest
    small = jnp.concatenate(
        [row_params.reshape(-1), qv_bias.reshape(-1), up_bias.reshape(-1)]
    )[None]

    def small_hop(values, mask):
        return ordered(values, mask, (dp_at * tensor_size + tensor_at) & mask != 0, 0)

    small_hops = bits_of(devices)
    small = small_hop(small, small_hops[0])
    small = tick(small, early)
    tokens_here = cross(tokens_in)
    first_stage = fetches_of(blocks_of(0, 1))
    next_fetches = []
    if layers > 1:
        next_fetches = fetches_of(blocks_of(1, 0))
    first_stage = first_stage + next_fetches
    small = small_hop(small, small_hops[1])
    small, tokens_here, first_blocks = tick(
        (small, tokens_here, [chain.block for chain in first_stage]), early
    )
    for chain, block in zip(first_stage, first_blocks):
        chain.block = block
        chain.send()
    stream = group_rows(tokens_here)
    small = small_hop(small, small_hops[2])
    small, stream = tick((small, stream), early)
    stream = to_local(stream).astype(F32)
    for mask in small_hops[3:]:
        small = small_hop(small, mask)
    later_others, small = tick(([chain.other for chain in first_stage], small), early)
    for chain, other in zip(first_stage, later_others):
        chain.other = other
    while early[0].place < steps:
        for chain in early:
            chain.take()

    row_size, qv_size = row_params.size, qv_bias.size
    rows_every = to_local(
        small[:, :row_size]
        .reshape(devices, layers, 6, -1)
        .transpose(1, 2, 0, 3)
        .reshape(layers, 6, features)
        .astype(F32)
    )

    def local_units(values, kinds):
        values = values.reshape(dp_size, spans, inner_size, layers, kinds, -1)
        values = lax.dynamic_slice_in_dim(values, core * pairs, pairs, 0)
        values = lax.dynamic_slice_in_dim(values, inner, 1, 2)[:, :, 0]
        blocks = [
            lax.dynamic_slice_in_dim(values, span ^ offset, 1, 1)[:, 0] for offset in range(spans)
        ]
        values = jnp.stack(blocks)
        return values.transpose(2, 3, 0, 1, 4).reshape(layers, kinds, -1).astype(F32)

    qv_local = local_units(small[:, row_size : row_size + qv_size], 2)
    up_bias_local = local_units(small[:, row_size + qv_size :], 1)[:, 0]

    span_at = jnp.stack([span ^ offset for offset in range(spans)])
    heads_at = (span_at * inner_size + inner)[:, None] * (2 * heads_half) + core * heads_half
    heads_at = heads_at + jnp.arange(heads_half, dtype=jnp.int32)[None]
    slopes = (2.0 ** (-8.0 * (heads_at.astype(F32) + 1.0) / HEADS)).reshape(-1, 2)

    own_segment = lax.dynamic_slice_in_dim(segment_ids, span // 2, 1, 0)
    seg_row = jnp.where(core == span % 2, own_segment, swap(own_segment, core_mask))
    seg_col = seg_row.reshape(-1, 1)

    fetches = [early + first_stage[:2], first_stage[2:]]
    stages = [early, first_stage]
    for number in range(1, layers):
        late = fetches_of(blocks_of(number, 1))
        fetches[number] = fetches[number] + late
        if number + 1 < layers:
            fetches.append(fetches_of(blocks_of(number + 1, 0)))
            late = late + fetches[number + 1]
        stages.append(late)
    for before, after in zip(stages[1:-1], stages[2:]):
        held = lax.optimization_barrier(
            ([chain.other for chain in before], [chain.block for chain in after])
        )
        for chain, other in zip(before, held[0]):
            chain.other = other
        for chain, block in zip(after, held[1]):
            chain.block = block
            chain.send()

    stash = []
    normed = layer_norm(stream, rows_every[0, 0], rows_every[0, 1]).astype(BF16)
    for number in range(layers):
        rows = rows_every[number]
        stage = stages[number + 1]
        weights = [chain.block for chain in fetches[number]]
        weights = weights[: len(weights) - 2] + [None, None]
        biases = (qv_local[number, 0], jnp.zeros_like(qv_local[number, 0]), qv_local[number, 1])
        if number:
            biases = (jnp.concatenate(biases),)
        packed = [
            (jnp.dot(normed, weight, preferred_element_type=F32) + bias).astype(BF16)
            for weight, bias in zip(weights[:-3], biases)
        ]
        if number == 0:
            packed = tick(packed, stage)
            packed, cotangent = lax.optimization_barrier((packed, cotangent))
            upstream_low = cross(cotangent)
        attended = attention_forward(packed, seg_col, seg_row, slopes)
        if number == 0:
            attended, upstream_low = tick((attended, upstream_low), stage)
            upstream_low = group_rows(upstream_low)
        middle = stream + (
            group_sum(jnp.dot(attended, weights[-3], preferred_element_type=F32)) + rows[2]
        )
        normed_two = layer_norm(middle, rows[3], rows[4]).astype(BF16)
        if number == 0:
            normed_two, upstream_low = lax.optimization_barrier((normed_two, upstream_low))
        while stage[0].place + 1 < steps:
            normed_two = tick(normed_two, stage)
        following = stages[number + 2] if number + 2 < len(stages) else []
        if following:
            normed_two = tick(normed_two, stage)
            weights_two, others = lax.optimization_barrier(
                ([chain.block for chain in stage], [chain.other for chain in following])
            )
            for chain, block in zip(stage, weights_two):
                chain.block = block
            for chain, other in zip(following, others):
                chain.other = other
                chain.take()
        else:
            for chain in stage:
                chain.take()
        weights = [chain.block for chain in fetches[number]]
        pre_gelu = (
            jnp.dot(normed_two, weights[-2], preferred_element_type=F32) + up_bias_local[number]
        )
        hidden = gelu_tanh(pre_gelu).astype(BF16)
        if following:
            hidden = tick(hidden, following)
        stash.append(
            (stream, normed, packed, attended, middle, normed_two, pre_gelu, hidden, weights)
        )
        stream = middle + (
            group_sum(jnp.dot(hidden, weights[-1], preferred_element_type=F32)) + rows[5]
        )
        if number + 1 < layers:
            after = rows_every[number + 1]
            normed = layer_norm(stream, after[0], after[1]).astype(BF16)
            if following[0].place + 1 < steps:
                normed = tick(normed, following)

    def give_back(values):
        at = (core * inner_size + inner) * shard_rows
        return cross(lax.dynamic_slice_in_dim(from_local(values), at, shard_rows, 0))

    output = give_back(stream.astype(BF16))

    upstream = to_local(upstream_low).astype(F32)
    reductions = [None] * layers
    small_grads = [None] * layers
    running = []
    for number in reversed(range(layers)):
        (
            stream_in,
            normed,
            packed,
            attended,
            middle,
            normed_two,
            pre_gelu,
            hidden,
            weights,
        ) = stash[number]
        rows = rows_every[number]
        apart = len(packed) == 3

        down_bias_grad = jnp.sum(upstream, axis=0)
        down_in = upstream.astype(BF16)
        down_chain = Reduce(down_in, hidden, 1, 1)
        hidden_grad = dot_nt(down_in, weights[-1])
        pre_grad = jax.vjp(gelu_tanh, pre_gelu)[1](hidden_grad)[0]
        up_bias_grad = jnp.sum(pre_grad, axis=0)
        pre_low = pre_grad.astype(BF16)
        pre_low = advance(pre_low, running)
        up_chain = Reduce(normed_two, pre_low, 0, 0)
        normed_two_grad = group_sum(dot_nt(pre_low, weights[-2]))
        middle_grad, gain_two_grad, shift_two_grad = norm_back(middle, rows[3], normed_two_grad)
        middle_grad = middle_grad + upstream
        out_bias_grad = jnp.sum(middle_grad, axis=0)
        out_in = middle_grad.astype(BF16)
        attended_grad = dot_nt(out_in, weights[-3]).astype(BF16)
        attended_grad = advance(attended_grad, running if number else running + [down_chain])
        out_chain = Reduce(out_in, attended, 1, 2)
        packed_grad, qv_sums = attention_backward(packed, attended_grad, seg_col, seg_row, slopes)
        packed_grad = advance(packed_grad, running + [down_chain, up_chain, out_chain])
        if apart:
            qkv_chains = [Reduce(normed, packed_grad[at], 0, at) for at in range(3)]
            normed_grad = (
                dot_nt(packed_grad[0], weights[0])
                + dot_nt(packed_grad[1], weights[1])
                + dot_nt(packed_grad[2], weights[2])
            )
        else:
            beside = jnp.concatenate([packed_grad[at] for at in range(3)], axis=1)
            qkv_chains = [Reduce(normed, beside, 0, 2, 3)]
            normed_grad = dot_nt(beside, weights[0])
        normed_grad = group_sum(normed_grad)
        stream_grad, gain_one_grad, shift_one_grad = norm_back(stream_in, rows[0], normed_grad)
        upstream = middle_grad + stream_grad
        if number:
            upstream = advance(upstream, running + [down_chain, up_chain, out_chain])
        running = running + [down_chain, up_chain, out_chain] + qkv_chains
        reductions[number] = qkv_chains + [out_chain, up_chain, down_chain]

        row_grads = from_local(
            jnp.stack(
                [
                    gain_one_grad,
                    shift_one_grad,
                    out_bias_grad,
                    gain_two_grad,
                    shift_two_grad,
                    down_bias_grad,
                ]
            )
        )
        qv_units = qv_sums.transpose(1, 0, 2).reshape(2, spans, half_width)
        units = jnp.concatenate(
            [qv_units.transpose(1, 0, 2).reshape(spans, -1), up_bias_grad.reshape(spans, -1)],
            axis=1,
        )
        units = jnp.concatenate(
            [
                lax.dynamic_slice_in_dim(units, span ^ true_span, 1, 0)
                for true_span in range(spans)
            ],
            axis=0,
        )
        small_grads[number] = jnp.concatenate([row_grads.reshape(-1), units.reshape(-1)])
    def own_grads(number):
        found = [chain.result for chain in reductions[number]]
        low, high = join_cores(jnp.concatenate(found[:-3], axis=1), 0)
        row_count = low.shape[0]
        qkv_own = jnp.concatenate(
            [low.reshape(row_count, 3, half_width), high.reshape(row_count, 3, half_width)], axis=2
        ).transpose(1, 0, 2)
        return (
            qkv_own,
            jnp.concatenate(join_cores(found[-3], 1), axis=0),
            jnp.concatenate(join_cores(found[-2], 0), axis=1),
            jnp.concatenate(join_cores(found[-1], 1), axis=0),
        )

    upstream = advance(upstream, [chain for chains in reductions[1:] for chain in chains])
    weight_grads = [
        own_grads(number) if all(chain.place > steps for chain in reductions[number]) else None
        for number in range(layers)
    ]
    summed = jnp.stack(small_grads)
    upstream, summed, weight_grads = lax.optimization_barrier((upstream, summed, weight_grads))
    grad_input = give_back(upstream.astype(BF16))
    small_masks = [span_masks[bit] for bit in span_bits] + [pair_masks[bit] for bit in pair_bits]
    running = [chain for chain in running if chain.place <= steps]
    while running or small_masks:
        if small_masks:
            passed = swap(summed, small_masks[0])
        passed = advance(passed, running)
        if small_masks:
            summed = summed + passed
            small_masks = small_masks[1:]
        running = [chain for chain in running if chain.place <= steps]
    weight_grads = [
        own_grads(number) if weight_grads[number] is None else weight_grads[number]
        for number in range(layers)
    ]

    row_total = 6 * features
    own = features // devices
    row_summed = lax.dynamic_slice_in_dim(
        summed[:, :row_total].reshape(layers, 6, features),
        (dp_at * tensor_size + tensor_at) * own,
        own,
        2,
    )
    units = summed[:, row_total:].reshape(layers, spans, -1)
    units = lax.dynamic_slice_in_dim(units, span, 1, 1)[:, 0]
    other_units = swap(units, core_mask)
    units = jnp.where(core_one == (dp_at >= pairs), units, other_units)
    place = dp_at % pairs
    qv_part = units[:, : 2 * half_width].reshape(layers, 2, pairs, -1)
    up_part = units[:, 2 * half_width :].reshape(layers, pairs, -1)
    qv_own = lax.dynamic_slice_in_dim(qv_part, place, 1, 2)[:, :, 0]
    up_own = lax.dynamic_slice_in_dim(up_part, place, 1, 1)[:, 0]

    joined = [
        jnp.stack([weight_grads[number][member] for number in range(layers)]) for member in range(4)
    ]
    return (
        output,
        grad_input.astype(F32),
        joined[0],
        qv_own,
        joined[1],
        joined[2],
        up_own,
        joined[3],
        row_summed,
    )


def solution(mesh):
    placed = (
        P(("dp", "tensor"), None),
        P("dp", None),
        P(None, None, "dp", "tensor"),
        P(None, None, ("tensor", "dp")),
        P(None, "tensor", "dp"),
        P(None, "dp", "tensor"),
        P(None, ("tensor", "dp")),
        P(None, "tensor", "dp"),
        P(None, None, ("dp", "tensor")),
        P(("dp", "tensor"), None),
    )
    return jax.shard_map(
        functools.partial(body, mesh.shape["dp"], mesh.shape["tensor"]),
        mesh=mesh,
        in_specs=placed,
        out_specs=(
            P(("dp", "tensor"), None),
            P(("dp", "tensor"), None),
            P(None, None, "dp", "tensor"),
            P(None, None, ("tensor", "dp")),
            P(None, "tensor", "dp"),
            P(None, "dp", "tensor"),
            P(None, ("tensor", "dp")),
            P(None, "tensor", "dp"),
            P(None, None, ("dp", "tensor")),
        ),
        check_vma=False,
    )
```
